256 devices in a mesh: ctx: 32 (over y, z), head: 8 (over x, core).
Axes of the slice: x: 4, y: 4, z: 8, core: 2. Of those that a mesh axis runs over, the one named last changes fastest.
Arguments:
- tokens: bfloat16 [16384, 2560], P('ctx', 'head'), may hold values from -6 to 6
- tangent_tokens: bfloat16 [16384, 2560], P('ctx', 'head'), may hold values from -6 to 6
- log_decay: float32 [16384, 80], P('ctx', 'head'), may hold values from -1.5 to 0, as said below
- tangent_decay: float32 [16384, 80], P('ctx', 'head'), may hold values from -0.096 to 0.096
- w_inner: bfloat16 [2560, 5120], P(None, 'head'), may hold values from -0.125 to 0.125
- w_bmat: bfloat16 [2560, 128], replicated, may hold values from -0.001953125 to 0.001953125
- w_cmat: bfloat16 [2560, 128], replicated, may hold values from -0.125 to 0.125
- conv_inner: float32 [4, 5120], P(None, 'head'), may hold values from -3 to 3
- conv_bc: float32 [4, 256], replicated, may hold values from -3 to 3
- skip_gain: float32 [80], P('head'), may hold values from 0.5 to 2
- w_out: bfloat16 [5120, 2560], P('head'), may hold values from -0.078125 to 0.078125
Outputs:
- output: bfloat16 [16384, 2560], P('ctx', 'head')
- output_tangent: bfloat16 [16384, 2560], P('ctx', 'head')
The draws below stay inside these ranges and needn't reach their ends.
Inputs may be any that keep to these rules, and one draw needn't show every extreme that they name: `log_decay`: negative; the natural logarithm of the factor by which each head's state is multiplied at each token.
All inputs are finite; a program needn't handle non-finite values.
Results may differ from the reference program's by a relative error of at most 0.019.
Values may be sent and summed in bfloat16 or wider, within the bound.
No kernel may reach another device: no remote copies, remote signals or barrier semaphores. Data moves between devices by JAX's collectives and lax.ppermute only.
A program may use at most 128 MiB of HBM per device.

```python
import jax
import jax.numpy as jnp
from jax import lax

D = 2560
HEADS = 80
HEAD_DIM = 64
STATE = 128
SPAN = 256
CONV = 4
TOK_DEV = 512
TOKENS = 16384
INNER = 5120
N_HEAD = 8


def draw_log_decay(key, part):
    key = jax.random.fold_in(key, 7)
    subkeys = jax.random.split(key, 7)
    lasting = jax.random.uniform(subkeys[0], (HEADS,)) < 0.3
    slow_rate = jax.random.uniform(subkeys[1], (HEADS,), jnp.float32, 0.1, 0.3) * 2.302585 / TOKENS
    medium_rate = jax.random.uniform(subkeys[2], (HEADS,), jnp.float32, 0.3, 0.7) / TOK_DEV
    decay_rate = jnp.where(lasting, slow_rate, medium_rate)
    blocks = TOKENS // TOK_DEV
    factor = jnp.exp(jax.random.uniform(subkeys[3], (blocks, 1, HEADS), jnp.float32, -0.7, 0.7))
    jitter = jax.random.uniform(subkeys[4], (blocks, TOK_DEV, HEADS), jnp.float32, 0.5, 1.5)
    steady = -(decay_rate[None, None, :] * factor * jitter).reshape(TOKENS, HEADS)
    places = jax.random.randint(subkeys[5], (3,), 0, TOKENS)
    struck = jnp.any(jnp.arange(TOKENS)[:, None] == places[None, :], axis=1)
    dropped = jax.random.uniform(subkeys[6], (TOKENS, HEADS), jnp.float32, 0.2, 0.5)
    return steady + jnp.where(struck[:, None], jnp.log(1.0 - dropped), 0.0)


def levels(stream_key, dims, shards, low, high):
    factor_of, own = 1.0, jax.random.fold_in(stream_key, 6)
    for dim, shards_of in shards:
        draws = jnp.exp(jax.random.uniform(jax.random.fold_in(own, dim), (shards_of,), jnp.float32, low / len(shards), high / len(shards)))
        factor_of = factor_of * jnp.repeat(draws, dims[dim] // shards_of).reshape([-1 if axis == dim else 1 for axis in range(len(dims))])
    return factor_of


def centred(own_key, dims, deviation, most, cuts=(), kind=jnp.bfloat16):
    result = jax.random.normal(own_key, dims, jnp.float32) * deviation
    if len(cuts) > 0:
        result = levels(own_key, dims, cuts, -0.22, 0.18) * result
    return jnp.clip(result, min=-most, max=most).astype(kind)


def setup_inputs(seed: int = 0) -> dict:
    keys = jax.random.split(jax.random.key(seed), 12)
    return {
        "tokens": centred(keys[0], (TOKENS, D), 1.0, 6.0, ((0, 32), (1, 8))),
        "tangent_tokens": centred(keys[1], (TOKENS, D), 1.0, 6.0, ((0, 32), (1, 8))),
        "log_decay": draw_log_decay(jax.random.fold_in(keys[11], 71), 0),
        "tangent_decay": centred(keys[3], (TOKENS, HEADS), 0.016, 0.096, ((0, 32), (1, 8)), jnp.float32),
        "w_inner": centred(keys[4], (D, INNER), D ** -0.5, 0.125, ((1, 8),)),
        "w_bmat": centred(keys[5], (D, STATE), (D * TOKENS * STATE // 512) ** -0.5, 0.001953125),
        "w_cmat": centred(keys[6], (D, STATE), D ** -0.5, 0.125),
        "conv_inner": centred(keys[7], (CONV, INNER), CONV ** -0.5, 3.0, ((1, 8),), jnp.float32),
        "conv_bc": centred(keys[8], (CONV, 2 * STATE), CONV ** -0.5, 3.0, (), jnp.float32),
        "skip_gain": jnp.clip(0.5 + 1.5 * jax.random.uniform(keys[9], (HEADS,), jnp.float32) ** levels(keys[9], (HEADS,), ((0, 8),), -0.2, 0.2), 0.5, 2.0),
        "w_out": centred(keys[10], (INNER, D), INNER ** -0.5, 0.078125, ((0, 8),)),
    }


def depthwise(padded, kernel):
    length = padded.shape[0] - kernel.shape[0] + 1
    summed = kernel[0] * padded[0:length]
    for offset in range(1, kernel.shape[0]):
        summed = summed + kernel[offset] * padded[offset:offset + length]
    return summed


def activate(values):
    return jax.nn.silu(values).astype(jnp.bfloat16)


def span_parts(inputs, writer, reader, decays):
    cumulative = jnp.cumsum(decays, axis=0)
    length = decays.shape[0]
    causal = lax.broadcasted_iota(jnp.int32, (length, length), 0) >= lax.broadcasted_iota(jnp.int32, (length, length), 1)
    differences = cumulative.T[:, :, None] - cumulative.T[:, None, :]
    weights = jnp.exp(jnp.where(causal[None], differences, -jnp.inf))
    scores = jnp.dot(reader, writer.T, preferred_element_type=jnp.float32)
    mixing = (weights * scores[None]).astype(jnp.bfloat16)
    within = jnp.einsum("hts,shp->thp", mixing.astype(jnp.float32), inputs.astype(jnp.float32), precision=lax.Precision.HIGHEST)
    remaining = jnp.exp(cumulative[-1][None, :] - cumulative)
    scaled = (inputs * remaining[:, :, None]).astype(jnp.bfloat16)
    block_state = jnp.einsum("shp,sn->hpn", scaled.astype(jnp.float32), writer.astype(jnp.float32), precision=lax.Precision.HIGHEST)
    return cumulative, within, block_state


def carried(reader, cumulative, initial):
    rounded = initial.astype(jnp.bfloat16)
    readout = jnp.einsum("tn,hpn->thp", reader.astype(jnp.float32), rounded.astype(jnp.float32), precision=lax.Precision.HIGHEST)
    return jnp.exp(cumulative)[:, :, None] * readout


def reference(tokens, tangent_tokens, log_decay, tangent_decay, w_inner, w_bmat, w_cmat, conv_inner, conv_bc, skip_gain, w_out):
    kernel = jnp.concatenate([conv_inner, conv_bc], 1)
    blocks = TOKENS // SPAN

    def sequence_mix(source, decays):
        projected = jnp.concatenate([
            jnp.dot(source, w_inner, preferred_element_type=jnp.float32).astype(jnp.bfloat16),
            jnp.dot(source, w_bmat, preferred_element_type=jnp.float32).astype(jnp.bfloat16),
            jnp.dot(source, w_cmat, preferred_element_type=jnp.float32).astype(jnp.bfloat16)], 1)
        padded = jnp.concatenate([jnp.zeros((CONV - 1, projected.shape[1]), jnp.bfloat16), projected], 0)
        mixed = activate(depthwise(padded, kernel))
        inputs = mixed[:, :INNER].reshape(blocks, SPAN, HEADS, HEAD_DIM)
        writer = mixed[:, INNER:INNER + STATE].reshape(blocks, SPAN, STATE)
        reader = mixed[:, INNER + STATE:].reshape(blocks, SPAN, STATE)
        decay_blocks = decays.reshape(blocks, SPAN, HEADS)

        def advance(initial, block):
            block_inputs, block_writer, block_reader, block_decays = block
            cumulative, within, block_state = span_parts(block_inputs, block_writer, block_reader, block_decays)
            combined = (within + carried(block_reader, cumulative, initial)) + skip_gain[None, :, None] * block_inputs
            following = jnp.exp(cumulative[-1])[:, None, None] * initial + block_state
            return following, combined.astype(jnp.bfloat16)

        start_state = jnp.zeros((HEADS, HEAD_DIM, STATE), jnp.float32)
        finished, outputs = lax.scan(advance, start_state, (inputs, writer, reader, decay_blocks))
        return outputs.reshape(TOKENS, INNER)

    inner, inner_tangent = jax.jvp(sequence_mix, (tokens, log_decay), (tangent_tokens, tangent_decay))
    group = INNER // N_HEAD

    def project(values):
        summed = jnp.zeros((TOKENS, D), jnp.float32)
        for member in range(N_HEAD):
            partial_term = jnp.dot(values[:, member * group:(member + 1) * group], w_out[member * group:(member + 1) * group], preferred_element_type=jnp.float32)
            summed = summed + lax.optimization_barrier(partial_term.astype(jnp.bfloat16)).astype(jnp.float32)
        return summed.astype(jnp.bfloat16)

    return project(inner), project(inner_tangent)
```

```python
import functools

import jax
import jax.numpy as jnp
from jax import lax
from jax.experimental import pallas as pl
from jax.experimental.pallas import tpu as pltpu
from jax.sharding import PartitionSpec as P

HEAD_DIM = 64
SPAN = 256
MIB = 1 << 20
BF16 = jnp.bfloat16
F32 = jnp.float32
HIGHEST = lax.Precision.HIGHEST

NN = (((1,), (0,)), ((), ()))
NT = (((1,), (1,)), ((), ()))
TN = (((0,), (0,)), ((), ()))


def mm(a, b, dims=NN, precision=None):
    return lax.dot_general(a, b, dims, precision=precision, preferred_element_type=F32)


def call(body, out, scratch=(), flops=0, bytes_accessed=0, smem=(), count=0, limit=40):
    in_specs = [
        pl.BlockSpec(memory_space=pltpu.SMEM if i in smem else pltpu.VMEM) for i in range(count)
    ]
    out_specs = jax.tree.map(lambda _: pl.BlockSpec(memory_space=pltpu.VMEM), out)
    return pl.pallas_call(
        body,
        out_shape=out,
        in_specs=in_specs,
        out_specs=out_specs,
        scratch_shapes=list(scratch),
        cost_estimate=pl.CostEstimate(
            flops=flops, bytes_accessed=bytes_accessed, transcendentals=0
        ),
        compiler_params=pltpu.CompilerParams(vmem_limit_bytes=limit * MIB),
    )


def spread(rows, width):
    head = lax.broadcasted_iota(jnp.int32, (rows, width), 0)
    lane = lax.broadcasted_iota(jnp.int32, (rows, width), 1)
    return jnp.where(lane // HEAD_DIM == head, 1.0, 0.0).astype(F32)


def decay_body(dec, cum, cumd, rem, remd, ecum, cum_t, cumd_t, vec, tot):
    s = lax.broadcasted_iota(jnp.int32, (SPAN, SPAN), 0)
    t = lax.broadcasted_iota(jnp.int32, (SPAN, SPAN), 1)
    upper = jnp.where(s <= t, 1.0, 0.0).astype(F32)
    lower = jnp.where(t <= s, 1.0, 0.0).astype(F32)
    ends = []
    for b in range(dec.shape[1] // SPAN):
        lanes = slice(b * SPAN, (b + 1) * SPAN)
        both = dec[:, lanes]
        c = mm(both, upper, NN, HIGHEST)
        c_t = mm(lower, both, NT, HIGHEST)
        p, d = c[:16], c[16:]
        cum[:, lanes] = p
        cumd[:, lanes] = d
        ecum[:, lanes] = jnp.exp(p)
        r = jnp.exp(p[:, SPAN - 1 :] - p)
        rem[:, lanes] = r
        remd[:, lanes] = r * (d[:, SPAN - 1 :] - d)
        cum_t[lanes, :] = c_t[:, :16]
        cumd_t[lanes, :] = c_t[:, 16:]
        ends.append(c_t[SPAN - 1 :, :])
    rows = jnp.concatenate(
        [ends[0][:, :16], ends[0][:, 16:], ends[1][:, :16], ends[1][:, 16:]]
        + [jnp.zeros((4, 16), F32)],
        0,
    )
    wide = mm(rows, spread(16, vec.shape[1]), NN, HIGHEST)
    row = lax.broadcasted_iota(jnp.int32, wide.shape, 0)
    vec[...] = jnp.where((row == 0) | (row == 2), jnp.exp(wide), wide)
    total = ends[0] + ends[1]
    tot[...] = jnp.zeros(tot.shape, F32)
    tot[0:1, 0:16] = total[:, :16]
    tot[1:2, 0:16] = total[:, 16:]


def totals_body(total, slope, retain_out, slope_out):
    one_hot = spread(total.shape[1], retain_out.shape[1])
    retain_out[...] = jnp.exp(mm(total[...], one_hot, NN, HIGHEST))
    slope_out[...] = mm(slope[...], one_hot, NN, HIGHEST)


def project(order, pieces, w_t, full, ext, halo):
    rows = pieces[0].shape[0]
    for i, piece in enumerate(pieces):
        full[pl.ds(pl.multiple_of(order[i] * rows, rows), rows), :] = piece[...]
    margin = halo.shape[1]
    ext[:, :margin] = halo[...].astype(F32)
    for b in range(full.shape[1] // SPAN):
        summed = mm(w_t[...], full[:, b * SPAN : (b + 1) * SPAN])
        ext[:, margin + b * SPAN : margin + (b + 1) * SPAN] = summed.astype(BF16).astype(F32)


def conv_slab(ext, taps, rows, margin):
    slab = ext[rows, :]
    count = taps.shape[1]
    kernel = taps[rows, :]
    summed = None
    for k in range(count):
        back = count - 1 - k
        moved = pltpu.roll(slab, back, 1) if back else slab
        term = kernel[:, k : k + 1] * moved[:, margin:]
        summed = term if summed is None else summed + term
    return summed


def primal_body(order, *refs):
    pieces, (w_t, halo, taps, mixed, gate, full, ext) = refs[:8], refs[8:]
    project(order, pieces, w_t, full, ext, halo)

    @pl.loop(0, mixed.shape[0] // 64)
    def _(i):
        rows = pl.ds(pl.multiple_of(i * 64, 64), 64)
        v = conv_slab(ext, taps, rows, halo.shape[1])
        sig = 1.0 / (1.0 + jnp.exp(-v))
        mixed[rows, :] = (v * sig).astype(BF16)
        gate[rows, :] = sig * (1.0 + v * (1.0 - sig))


def interleave(back):
    r = lax.broadcasted_iota(jnp.int32, (256, 256), 1 if back else 0)
    k = lax.broadcasted_iota(jnp.int32, (256, 256), 0 if back else 1)
    source = 4 * (r >> 3) + (r & 3) + 128 * ((r >> 2) & 1)
    return jnp.where(k == source, 1.0, 0.0).astype(BF16)


def tangent_body(order, *refs):
    pieces, refs = refs[:8], refs[8:]
    (w_t, halo, taps, mixed, gate, rem, remd, vec) = refs[:8]
    (mixed_dot, message, state0, state0_dot, full, ext, scaled) = refs[8:]
    project(order, pieces, w_t, full, ext, halo)

    @pl.loop(0, mixed.shape[0] // 64)
    def _(i):
        rows = pl.ds(pl.multiple_of(i * 64, 64), 64)
        v = conv_slab(ext, taps, rows, halo.shape[1])
        mixed_dot[rows, :] = (gate[rows, :] * v).astype(BF16)

    width = vec.shape[1]
    states = []
    for b in range(2):
        lanes = slice(b * SPAN, (b + 1) * SPAN)
        for h in range(width // HEAD_DIM):
            rows = slice(h * HEAD_DIM, (h + 1) * HEAD_DIM)
            value = mixed[rows, lanes].astype(F32)
            r = rem[h : h + 1, lanes]
            scaled[rows, SPAN:] = (value * r).astype(BF16)
            scaled[rows, :SPAN] = (
                mixed_dot[rows, lanes].astype(F32) * r + value * remd[h : h + 1, lanes]
            ).astype(BF16)
        writer = mixed[width : width + 128, lanes]
        writer_dot = mixed_dot[width : width + 128, lanes]
        state = mm(writer, scaled[:, SPAN:], NT)
        state_dot = mm(writer, scaled[:, :SPAN], NT) + mm(writer_dot, scaled[:, SPAN:], NT)
        states.append((state, state_dot))
    (s0, d0), (s1, d1) = states
    state0[...] = s0
    state0_dot[...] = d0
    retain = vec[2:3, :]
    own = retain * s0 + s1
    own_dot = retain * (d0 + vec[3:4, :] * s0) + d1
    stacked = jnp.concatenate([own.astype(BF16), own_dot.astype(BF16)], 0)
    message[...] = mm(interleave(False), stacked).astype(BF16)


def within_body(mixed, mixed_dot, cum, cumd, cum_t, cumd_t, gain, within, within_dot, sc, scd):
    width = within.shape[0]
    state = (mixed.shape[0] - width) // 2
    s = lax.broadcasted_iota(jnp.int32, (SPAN, SPAN), 0)
    t = lax.broadcasted_iota(jnp.int32, (SPAN, SPAN), 1)
    causal = s <= t
    for b in range(2):
        lanes = slice(b * SPAN, (b + 1) * SPAN)
        writer, reader = mixed[width : width + state, lanes], mixed[width + state :, lanes]
        writer_dot = mixed_dot[width : width + state, lanes]
        reader_dot = mixed_dot[width + state :, lanes]
        sc[...] = mm(writer, reader, TN)
        scd[...] = mm(writer_dot, reader, TN) + mm(writer, reader_dot, TN)
        for h in range(width // HEAD_DIM):
            rows = slice(h * HEAD_DIM, (h + 1) * HEAD_DIM)
            diff = cum[h : h + 1, lanes] - cum_t[lanes, h : h + 1]
            diff_dot = cumd[h : h + 1, lanes] - cumd_t[lanes, h : h + 1]
            weight = jnp.exp(jnp.where(causal, diff, -jnp.inf))
            mix = (weight * sc[...]).astype(BF16)
            mix_dot = (weight * (scd[...] + diff_dot * sc[...])).astype(BF16)
            value, value_dot = mixed[rows, lanes], mixed_dot[rows, lanes]
            both = mm(jnp.concatenate([value, value_dot], 0), mix)
            other = mm(value, mix_dot)
            skip = gain[0:1, h : h + 1]
            within[rows, lanes] = both[:HEAD_DIM] + skip * value.astype(F32)
            within_dot[rows, lanes] = (both[HEAD_DIM:] + other) + skip * value_dot.astype(F32)


def scan_body(arrived, retain, slope, leaving):
    steps, rows, width = arrived.shape
    low = lax.broadcasted_iota(jnp.int32, (rows, width), 0) >= rows // 2
    state = jnp.zeros((rows, width), F32)
    for j in range(steps):
        leaving[j] = state.astype(BF16)
        r = retain[j : j + 1, :]
        pushed = jnp.where(low, pltpu.roll(state, rows // 2, 0) * slope[j : j + 1, :], 0.0)
        state = r * (state + pushed) + arrived[j].astype(F32)


def out_product(order, w_t, gathered, values, out):
    count, rows, _ = out.shape
    for d in range(count):
        gathered[d * rows : (d + 1) * rows, :] = w_t[
            pl.ds(pl.multiple_of(order[d] * rows, rows), rows), :
        ]
    for b in range(values.shape[1] // SPAN):
        lanes = slice(b * SPAN, (b + 1) * SPAN)
        result = mm(gathered[...], values[:, lanes]).astype(BF16)
        for d in range(count):
            out[d, :, lanes] = result[d * rows : (d + 1) * rows]


def readout_body(
    order, entry, mixed, mixed_dot, within, within_dot, cumd, ecum, vec, state0, state0_dot, w_t,
    inner, inner_dot, out, gathered
):
    width = within.shape[0]
    n = state0.shape[0]
    both = mm(interleave(True), entry[...])
    for b in range(2):
        lanes = slice(b * SPAN, (b + 1) * SPAN)
        rounded = both.astype(BF16)
        reader, reader_dot = mixed[width + n :, lanes], mixed_dot[width + n :, lanes]
        read = mm(rounded[:n], reader, TN)
        read_dot = mm(rounded[:n], reader_dot, TN) + mm(rounded[n:], reader, TN)
        for h in range(width // HEAD_DIM):
            rows = slice(h * HEAD_DIM, (h + 1) * HEAD_DIM)
            e = ecum[h : h + 1, lanes]
            d = cumd[h : h + 1, lanes]
            inner[rows, lanes] = (within[rows, lanes] + e * read[rows]).astype(BF16)
            inner_dot[rows, lanes] = (
                within_dot[rows, lanes] + e * (read_dot[rows] + d * read[rows])
            ).astype(BF16)
        if b == 0:
            retain, slope = vec[0:1, :], vec[1:2, :]
            first, second = both[:n], both[n:]
            both = jnp.concatenate(
                [
                    retain * first + state0[...],
                    retain * (second + slope * first) + state0_dot[...],
                ],
                0,
            )
    out_product(order, w_t, gathered, inner, out)


def product_body(order, w_t, values, out, gathered):
    out_product(order, w_t, gathered, values, out)


def add_body(kept, received, *outs):
    for d, out in enumerate(outs):
        out[...] = (kept[d].astype(F32) + received[d].astype(F32)).astype(BF16)


def total_body(a, b, c, d, out):
    out[...] = (
        (a[...].astype(F32) + b[...].astype(F32)) + (c[...].astype(F32) + d[...].astype(F32))
    ).astype(BF16)


def on_device(
    tokens,
    tangent_tokens,
    log_decay,
    tangent_decay,
    w_inner,
    w_bmat,
    w_cmat,
    conv_inner,
    conv_bc,
    skip_gain,
    w_out,
):
    length, piece = tokens.shape
    width = w_inner.shape[1]
    state_len = w_bmat.shape[1]
    channels = width + 2 * state_len
    heads = width // HEAD_DIM
    model = w_inner.shape[0]
    n_ctx, n_head = lax.axis_size("ctx"), lax.axis_size("head")
    chips = n_head // 2
    margin = conv_inner.shape[0] - 1
    shape = jax.ShapeDtypeStruct
    place = lax.axis_index("head")
    chip, core = place // 2, place % 2

    def along(values, distance):
        route = [
            (2 * i + j, 2 * ((i + distance) % chips) + j) for i in range(chips) for j in range(2)
        ]
        return lax.ppermute(values, "head", route)

    def swap(values):
        return lax.ppermute(values, "head", [(i, i ^ 1) for i in range(n_head)])

    first, second = tokens.T, tangent_tokens.T
    first_up, first_down = along(first, 1), along(first, -1)
    second_up, second_down = along(second, 1), along(second, -1)
    first_far = along(first_up, 1)
    second_far = along(second_down, -1)
    firsts = [first, first_up, first_down, first_far]
    seconds = [second, second_up, second_down, second_far]
    firsts = firsts + [swap(v) for v in firsts]
    seconds = seconds + [swap(v) for v in seconds]
    chip_of = [chip, chip - 1, chip + 1, chip + 2]
    order = jnp.stack(
        [(i + chips) % chips * 2 + core for i in chip_of]
        + [(i + chips) % chips * 2 + (1 - core) for i in chip_of]
    ).astype(jnp.int32)

    gap = jnp.zeros((1, piece), BF16)
    edge = jnp.concatenate([tokens[length - margin :], gap, tangent_tokens[length - margin :], gap])
    edge = lax.ppermute(edge, "ctx", [(i, i + 1) for i in range(n_ctx - 1)])
    edge = lax.all_to_all(jnp.broadcast_to(edge[None], (n_head, *edge.shape)), "head", 0, 0)
    edge = edge.transpose(1, 0, 2).reshape(edge.shape[1], model)
    fill = jnp.zeros((128 - margin, model), BF16)
    before = jnp.concatenate([fill, edge[:margin], fill, edge[margin + 1 : 2 * margin + 1]])
    w_t = jnp.concatenate([w_inner, w_bmat, w_cmat], 1).T
    halo = jnp.dot(w_t, before.T, preferred_element_type=F32).astype(BF16)
    taps = jnp.concatenate([conv_inner, conv_bc], 1).T
    wout_t = w_out.T

    pad = ((0, 16 - heads), (0, 0))
    dec = jnp.concatenate([jnp.pad(log_decay.T, pad), jnp.pad(tangent_decay.T, pad)], 0)
    rows = shape((16, length), F32)
    columns = shape((length, 16), F32)
    cum, cumd, rem, remd, ecum, cum_t, cumd_t, vec, tot = call(
        decay_body,
        [rows] * 5 + [columns] * 2 + [shape((8, width), F32), shape((8, 128), F32)],
        count=1,
        flops=10**8,
        bytes_accessed=10**6,
    )(dec)
    tots = lax.all_to_all(jnp.broadcast_to(tot[None], (n_ctx, *tot.shape)), "ctx", 0, 0)
    retain, slope = call(
        totals_body, [shape((n_ctx, width), F32)] * 2, count=2, flops=10**7, bytes_accessed=10**6
    )(tots[:, 0], tots[:, 1])

    scratch = [pltpu.VMEM((model, length), BF16), pltpu.VMEM((channels, length + 128), F32)]
    cost = dict(flops=2 * channels * model * length, bytes_accessed=12 * MIB)
    mixed, gate = call(
        primal_body,
        [shape((channels, length), BF16), shape((channels, length), F32)],
        scratch,
        count=12,
        smem=(0,),
        **cost,
    )(order, *firsts, w_t, halo[:, :128], taps)
    state = shape((state_len, width), F32)
    mixed_dot, message, state0, state0_dot = call(
        tangent_body,
        [shape((channels, length), BF16), shape((2 * state_len, width), BF16), state, state],
        scratch + [pltpu.VMEM((width, 2 * SPAN), BF16)],
        count=17,
        smem=(0,),
        **cost,
    )(order, *seconds, w_t, halo[:, 128:], taps, mixed, gate, rem, remd, vec)

    share = 2 * state_len // n_ctx
    arrived = lax.all_to_all(message.reshape(n_ctx, share, width), "ctx", 0, 0)
    gains = jnp.pad(skip_gain[None], ((0, 0), (0, 16 - heads)))
    wide = shape((width, length), F32)
    within, within_dot = call(
        within_body,
        [wide, wide],
        [pltpu.VMEM((SPAN, SPAN), F32)] * 2,
        count=7,
        flops=10**10 // 2,
        bytes_accessed=8 * MIB,
    )(mixed, mixed_dot, cum, cumd, cum_t, cumd_t, gains)
    leaving = call(
        scan_body, shape((n_ctx, share, width), BF16), count=3, flops=10**8, bytes_accessed=MIB
    )(arrived, retain, slope)
    entry = lax.all_to_all(leaving, "ctx", 0, 0).reshape(2 * state_len, width)

    ring = [(chip + d) % chips for d in range(chips)]
    send_order = jnp.stack([i * 2 + (1 - core) for i in ring]).astype(jnp.int32)
    keep_order = jnp.stack([i * 2 + core for i in ring]).astype(jnp.int32)
    half = shape((chips, piece, length), BF16)
    gathered = [pltpu.VMEM((chips * piece, width), BF16)]
    cost = dict(flops=2 * chips * piece * width * length, bytes_accessed=6 * MIB)
    values = shape((width, length), BF16)
    inner, inner_dot, send = call(
        readout_body, [values, values, half], gathered, count=12, smem=(0,), **cost
    )(
        send_order, entry, mixed, mixed_dot, within, within_dot, cumd, ecum, vec, state0,
        state0_dot, wout_t,
    )
    product = call(product_body, half, gathered, count=3, smem=(0,), **cost)
    add = call(
        add_body, [shape((piece, length), BF16)] * chips, count=2, bytes_accessed=4 * MIB, flops=10**6
    )
    total = call(
        total_body, shape((piece, length), BF16), count=4, bytes_accessed=2 * MIB, flops=10**6
    )

    def finish(send, values):
        received = swap(send)
        own, *others = add(product(keep_order, wout_t, values), received)
        return total(own, *[along(v, d + 1) for d, v in enumerate(others)]).T

    send_dot = product(send_order, wout_t, inner_dot)
    return finish(send, inner), finish(send_dot, inner_dot)


def solution(mesh):
    in_specs = (
        P("ctx", "head"),
        P("ctx", "head"),
        P("ctx", "head"),
        P("ctx", "head"),
        P(None, "head"),
        P(),
        P(),
        P(None, "head"),
        P(),
        P("head"),
        P("head", None),
    )
    out_specs = (P("ctx", "head"), P("ctx", "head"))
    return jax.shard_map(
        on_device, mesh=mesh, in_specs=in_specs, out_specs=out_specs, check_vma=False
    )
```

```python
import functools

import jax
import jax.numpy as jnp
from jax import lax
from jax.experimental import pallas as pl
from jax.experimental.pallas import tpu as pltpu
from jax.sharding import PartitionSpec as P

HEAD_DIM = 64
SPAN = 256
MIB = 1 << 20
BIG = 56
BF16 = jnp.bfloat16
F32 = jnp.float32
HIGHEST = lax.Precision.HIGHEST

NN = (((1,), (0,)), ((), ()))
NT = (((1,), (1,)), ((), ()))
TN = (((0,), (0,)), ((), ()))


def mm(a, b, dims=NN, precision=None):
    return lax.dot_general(a, b, dims, precision=precision, preferred_element_type=F32)


def call(body, out, scratch=(), smem=(), near=(), held=(), pinned=(), count=0, work=(0, 0), limit=16):
    outs = list(out)
    n_out, n_scratch = len(outs), len(scratch)
    far = [i for i in range(count) if i not in smem and i not in held and i not in near]
    far_out = list(range(n_out)) if pinned is True else list(pinned)

    def kernel(*refs):
        ins, res = list(refs[:count]), list(refs[count : count + n_out])
        rest = refs[count + n_out :]
        own, rest = list(rest[:n_scratch]), list(rest[n_scratch:])
        copies, late = [], []
        for k, i in enumerate(far):
            copies.append(pltpu.make_async_copy(ins[i], rest[k], rest[-1].at[k]))
            ins[i] = rest[k]
        for k, i in enumerate(far_out, len(far)):
            late.append(pltpu.make_async_copy(rest[k], res[i], rest[-1].at[k]))
            res[i] = rest[k]
        for copy in copies:
            copy.start()
        if held:
            body(copies, *ins, *res, *own)
        else:
            for copy in copies:
                copy.wait()
            body(*ins, *res, *own)
        for copy in late:
            copy.start()
        for copy in late:
            copy.wait()

    def space(i):
        return pltpu.SMEM if i in smem else pltpu.VMEM if i in near else pltpu.HBM

    def run(*args):
        assert len(args) == count
        buffers = [pltpu.VMEM(args[i].shape, args[i].dtype) for i in far]
        buffers += [pltpu.VMEM(outs[i].shape, outs[i].dtype) for i in far_out]
        if buffers:
            buffers.append(pltpu.SemaphoreType.DMA((len(buffers),)))
        return pl.pallas_call(
            kernel,
            out_shape=[
                pltpu.HBM(v.shape, v.dtype) if i in far_out else v for i, v in enumerate(outs)
            ],
            in_specs=[pl.BlockSpec(memory_space=space(i)) for i in range(count)],
            out_specs=[
                pl.BlockSpec(memory_space=pltpu.HBM if i in far_out else pltpu.VMEM)
                for i in range(n_out)
            ],
            scratch_shapes=list(scratch) + buffers,
            cost_estimate=pl.CostEstimate(
                flops=work[0], bytes_accessed=work[1], transcendentals=0
            ),
            compiler_params=pltpu.CompilerParams(vmem_limit_bytes=limit * MIB),
        )(*args)

    return run


def spread(rows, width):
    head = lax.broadcasted_iota(jnp.int32, (rows, width), 0)
    lane = lax.broadcasted_iota(jnp.int32, (rows, width), 1)
    return jnp.where(lane // HEAD_DIM == head, 1.0, 0.0).astype(F32)


CUM, CUM_DOT, REM, REM_DOT, CUM_EXP = 0, 16, 32, 48, 64


def decay_body(dec, table, columns, vec, tail):
    s = lax.broadcasted_iota(jnp.int32, (SPAN, SPAN), 0)
    t = lax.broadcasted_iota(jnp.int32, (SPAN, SPAN), 1)
    upper = jnp.where(s <= t, 1.0, 0.0).astype(F32)
    lower = jnp.where(t <= s, 1.0, 0.0).astype(F32)
    ends = []
    for b in range(dec.shape[1] // SPAN):
        lanes = slice(b * SPAN, (b + 1) * SPAN)
        both = dec[:, lanes]
        c = mm(both, upper, NN, HIGHEST)
        c_t = mm(lower, both, NT, HIGHEST)
        p, d = c[:16], c[16:]
        table[CUM : CUM + 16, lanes] = p
        table[CUM_DOT : CUM_DOT + 16, lanes] = d
        table[CUM_EXP : CUM_EXP + 16, lanes] = jnp.exp(p)
        r = jnp.exp(p[:, SPAN - 1 :] - p)
        table[REM : REM + 16, lanes] = r
        table[REM_DOT : REM_DOT + 16, lanes] = r * (d[:, SPAN - 1 :] - d)
        columns[lanes, :] = c_t
        ends.append(c_t[SPAN - 1 :, :])
    rows = jnp.concatenate(
        [ends[0][:, :16], ends[0][:, 16:], ends[1][:, :16], ends[1][:, 16:]]
        + [jnp.zeros((4, 16), F32)],
        0,
    )
    wide = mm(rows, spread(16, vec.shape[1]), NN, HIGHEST)
    row = lax.broadcasted_iota(jnp.int32, wide.shape, 0)
    vec[...] = jnp.where((row == 0) | (row == 2), jnp.exp(wide), wide)
    rest = ends[0] + ends[1]
    tail[...] = jnp.zeros(tail.shape, F32)
    for i in range(3):
        term = rest.astype(BF16).astype(F32)
        tail[i : i + 1, 0:32] = term
        rest = rest - term


def edge_body(copies, first, second, out, last):
    for i, ref in enumerate((first, second)):
        pltpu.sync_copy(ref.at[:, ref.shape[1] - 128 :], last.at[i])
    row = lax.broadcasted_iota(jnp.int32, (16, 128), 0)
    lane = lax.broadcasted_iota(jnp.int32, (16, 128), 1)
    total = None
    for i in range(2):
        hit = (lane == row - 8 * i + 120) & (lane > 124) & (row >> 3 == i)
        term = mm(jnp.where(hit, 1.0, 0.0).astype(BF16), last[i], NT)
        total = term if total is None else total + term
    out[...] = total.astype(BF16)


def weight_body(w_inner, w_bmat, w_cmat, w_all):
    width, state = w_inner.shape[1], w_bmat.shape[1]
    w_all[:, :width] = w_inner[...]
    w_all[:, width : width + state] = w_bmat[...]
    w_all[:, width + state :] = w_cmat[...]


def gather(order, pieces, full, sems):
    rows = pieces[0].shape[0]
    arriving = [
        pltpu.make_async_copy(
            piece, full.at[pl.ds(pl.multiple_of(order[i] * rows, rows), rows), :], sems.at[i]
        )
        for i, piece in enumerate(pieces)
    ]
    for copy in arriving:
        copy.start()
    return arriving


def project(full, w_all, ext, halo):
    ext[0:8, :] = halo
    for b in range(full.shape[1] // SPAN):
        summed = mm(full[:, b * SPAN : (b + 1) * SPAN], w_all[...], TN)
        ext[8 + b * SPAN : 8 + (b + 1) * SPAN, :] = summed.astype(BF16).astype(F32)


CHUNK = 64


def convolve(ext, taps, b, store):
    count = taps.shape[0]
    for c in range(taps.shape[1] // 128):
        lanes = slice(c * 128, (c + 1) * 128)
        kernel = [jnp.broadcast_to(taps[k : k + 1, lanes], (CHUNK, 128)) for k in range(count)]
        for r in range(b * SPAN, (b + 1) * SPAN, CHUNK):
            summed = None
            for k in range(count):
                at = r + 9 - count + k
                term = kernel[k] * ext[at : at + CHUNK, lanes]
                summed = term if summed is None else summed + term
            store(slice(r, r + CHUNK), lanes, summed)


def turn(rows, out):
    s = lax.broadcasted_iota(jnp.int32, (SPAN, SPAN), 0)
    t = lax.broadcasted_iota(jnp.int32, (SPAN, SPAN), 1)
    one = jnp.where(s == t, 1.0, 0.0).astype(BF16)

    def block(b):
        lanes = slice(b * SPAN, (b + 1) * SPAN)
        out[:, lanes] = mm(rows[lanes, :], one, TN).astype(BF16)

    return block


def to_owners(values):
    n, width = values.shape
    halves = [values[:, : width // 2], values[:, width // 2 :]]
    stacked = jnp.stack([v.reshape(n // 8, 8, width // 2) for v in halves], 1)
    return stacked.reshape(2 * n, width // 2)


def from_owners(values):
    n, width = values.shape
    split = values.reshape(n // 16, 2, 8, width)
    return jnp.concatenate([split[:, i].reshape(n // 2, width) for i in range(2)], 1)


def primal_body(copies, order, *refs):
    pieces, (w_all, edge, taps, table, vec) = refs[:8], refs[8:13]
    mixed, gate, halo, state0, own, full, ext, rows, scaled, sems = refs[13:]
    arriving = gather(order, pieces, full, sems)
    for copy in copies:
        copy.wait()
    halo[...] = mm(edge[...], w_all[...]).astype(BF16).astype(F32)
    for copy in arriving:
        copy.wait()
    project(full, w_all, ext, halo[0:8, :])

    def store(at, lanes, v):
        sig = 1.0 / (1.0 + jnp.exp(-v))
        rows[at, lanes] = (v * sig).astype(BF16)
        gate[at, lanes] = sig * (1.0 + v * (1.0 - sig))

    block = turn(rows, mixed)
    for b in range(2):
        convolve(ext, taps, b, store)
        block(b)

    width = vec.shape[1]
    states = []
    for b in range(2):
        lanes = slice(b * SPAN, (b + 1) * SPAN)
        for h in range(width // HEAD_DIM):
            rows = slice(h * HEAD_DIM, (h + 1) * HEAD_DIM)
            value = mixed[rows, lanes].astype(F32)
            scaled[rows, :] = (value * table[REM + h : REM + h + 1, lanes]).astype(BF16)
        states.append(mm(mixed[width : width + 128, lanes], scaled[...], NT))
    state0[...] = states[0]
    own[...] = vec[2:3, :] * states[0] + states[1]


def tangent_body(copies, order, *refs):
    pieces, (w_all, halo, taps, table, vec) = refs[:8], refs[8:13]
    mixed, gate, state0, own, tail, mixed_dot, state0_dot, message = refs[13:21]
    full, ext, rows, scaled, sems = refs[21:]
    arriving = gather(order, pieces, full, sems)
    for copy in copies:
        copy.wait()
    for copy in arriving:
        copy.wait()
    project(full, w_all, ext, halo[8:16, :])

    def store(at, lanes, v):
        rows[at, lanes] = (gate[at, lanes] * v).astype(BF16)

    block = turn(rows, mixed_dot)
    for b in range(2):
        convolve(ext, taps, b, store)
        block(b)

    width = vec.shape[1]
    states = []
    for b in range(2):
        lanes = slice(b * SPAN, (b + 1) * SPAN)
        for h in range(width // HEAD_DIM):
            rows = slice(h * HEAD_DIM, (h + 1) * HEAD_DIM)
            value = mixed[rows, lanes].astype(F32)
            r = table[REM + h : REM + h + 1, lanes]
            scaled[rows, SPAN:] = (value * r).astype(BF16)
            scaled[rows, :SPAN] = (
                mixed_dot[rows, lanes].astype(F32) * r
                + value * table[REM_DOT + h : REM_DOT + h + 1, lanes]
            ).astype(BF16)
        writer = mixed[width : width + 128, lanes]
        writer_dot = mixed_dot[width : width + 128, lanes]
        states.append(mm(writer, scaled[:, :SPAN], NT) + mm(writer_dot, scaled[:, SPAN:], NT))
    state0_dot[...] = states[0]
    own_dot = vec[2:3, :] * (states[0] + vec[3:4, :] * state0[...]) + states[1]
    message[:, : width // 2] = to_owners(own[...]).astype(BF16)
    message[:, width // 2 : width] = to_owners(own_dot).astype(BF16)
    both = jnp.concatenate([tail[...], tail[...]], 0).astype(BF16)
    for j in range(message.shape[0] // 16):
        message[16 * j : 16 * j + 16, width:] = both


def within_body(mixed, mixed_dot, table, columns, gain, within, within_dot, sc, scd):
    width = within.shape[0]
    state = (mixed.shape[0] - width) // 2
    s = lax.broadcasted_iota(jnp.int32, (SPAN, SPAN), 0)
    t = lax.broadcasted_iota(jnp.int32, (SPAN, SPAN), 1)
    causal = s <= t
    for b in range(2):
        lanes = slice(b * SPAN, (b + 1) * SPAN)
        writer, reader = mixed[width : width + state, lanes], mixed[width + state :, lanes]
        writer_dot = mixed_dot[width : width + state, lanes]
        reader_dot = mixed_dot[width + state :, lanes]
        sc[...] = mm(writer, reader, TN)
        scd[...] = mm(writer_dot, reader, TN) + mm(writer, reader_dot, TN)
        for h in range(width // HEAD_DIM):
            rows = slice(h * HEAD_DIM, (h + 1) * HEAD_DIM)
            diff = table[CUM + h : CUM + h + 1, lanes] - columns[lanes, h : h + 1]
            diff_dot = (
                table[CUM_DOT + h : CUM_DOT + h + 1, lanes] - columns[lanes, 16 + h : 17 + h]
            )
            weight = jnp.exp(jnp.where(causal, diff, -jnp.inf))
            mix = (weight * sc[...]).astype(BF16)
            mix_dot = (weight * (scd[...] + diff_dot * sc[...])).astype(BF16)
            value, value_dot = mixed[rows, lanes], mixed_dot[rows, lanes]
            both = mm(jnp.concatenate([value, value_dot], 0), mix)
            other = mm(value, mix_dot)
            skip = gain[0:1, h : h + 1]
            within[rows, lanes] = both[:HEAD_DIM] + skip * value.astype(F32)
            within_dot[rows, lanes] = (both[HEAD_DIM:] + other) + skip * value_dot.astype(F32)


def unpack(half, width, which):
    lane = lax.broadcasted_iota(jnp.int32, (128, width), 0)
    head = lax.broadcasted_iota(jnp.int32, (128, width), 1) // HEAD_DIM + half * (width // HEAD_DIM)
    return jnp.where(lane == head + 16 * which, 1.0, 0.0).astype(BF16)


def scan_body(half, arrived, leaving, states, retain, slope):
    rows, whole = 8, leaving.shape[1]
    width = whole // 2
    steps = arrived.shape[0] // rows
    tails = arrived[:, whole:]
    for which, out in ((0, retain), (1, slope)):
        terms = mm(tails, unpack(half[0], width, which)).reshape(steps, rows, width)
        out[...] = (terms[:, 0] + terms[:, 1]) + terms[:, 2]
    retain[...] = jnp.exp(retain[...])
    states[...] = arrived[:, :whole].astype(F32)
    state = jnp.zeros((rows, width), F32)
    state_dot = jnp.zeros((rows, width), F32)
    for j in range(steps):
        own = slice(j * rows, (j + 1) * rows)
        arriving, arriving_dot = states[own, :width], states[own, width:]
        states[own, :width] = state
        states[own, width:] = state_dot
        r = retain[j : j + 1, :]
        state_dot = r * (state_dot + slope[j : j + 1, :] * state) + arriving_dot
        state = r * state + arriving
    leaving[...] = states[...].astype(BF16)


def arrange_body(order, w_t, keep, send):
    rows = w_t.shape[0] // order.shape[0]
    for d in range(order.shape[0] // 2):
        own = slice(d * rows, (d + 1) * rows)
        keep[own, :] = w_t[pl.ds(pl.multiple_of(order[2 * d] * rows, rows), rows), :]
        send[own, :] = w_t[pl.ds(pl.multiple_of(order[2 * d + 1] * rows, rows), rows), :]


def product_body(keep, received, own, other, *outs):
    rows = outs[0].shape[0]
    for b in range(own.shape[1] // SPAN):
        lanes = slice(b * SPAN, (b + 1) * SPAN)
        result = mm(keep[...], own[:, lanes]) + mm(received[...], other[:, lanes])
        for d, out in enumerate(outs):
            out[:, lanes] = result[d * rows : (d + 1) * rows].astype(BF16)


def read_body(arrived, reader, within, table, vec, state0, inner):
    width = within.shape[0]
    entry = from_owners(arrived[:, : width // 2].astype(F32))
    for b in range(2):
        lanes = slice(b * SPAN, (b + 1) * SPAN)
        read = mm(entry.astype(BF16), reader[:, lanes], TN)
        for h in range(width // HEAD_DIM):
            rows = slice(h * HEAD_DIM, (h + 1) * HEAD_DIM)
            e = table[CUM_EXP + h : CUM_EXP + h + 1, lanes]
            inner[rows, lanes] = (within[rows, lanes] + e * read[rows]).astype(BF16)
        if b == 0:
            entry = vec[0:1, :] * entry + state0[...]


def read_dot_body(arrived, readers, readers_dot, within, table, vec, s0, s0_dot, inner):
    width = within.shape[0]
    entry = from_owners(arrived[:, : width // 2].astype(F32))
    entry_dot = from_owners(arrived[:, width // 2 :].astype(F32))
    for b in range(2):
        lanes = slice(b * SPAN, (b + 1) * SPAN)
        reader, reader_dot = readers[:, lanes], readers_dot[:, lanes]
        rounded = entry.astype(BF16)
        read = mm(rounded, reader, TN)
        read_dot = mm(rounded, reader_dot, TN) + mm(entry_dot.astype(BF16), reader, TN)
        for h in range(width // HEAD_DIM):
            rows = slice(h * HEAD_DIM, (h + 1) * HEAD_DIM)
            e = table[CUM_EXP + h : CUM_EXP + h + 1, lanes]
            d = table[CUM_DOT + h : CUM_DOT + h + 1, lanes]
            inner[rows, lanes] = (
                within[rows, lanes] + e * (read_dot[rows] + d * read[rows])
            ).astype(BF16)
        if b == 0:
            retain, slope = vec[0:1, :], vec[1:2, :]
            entry_dot = retain * (entry_dot + slope * entry) + s0_dot[...]
            entry = retain * entry + s0[...]


def total_body(*refs):
    out = refs[-1]
    summed = refs[0][...].astype(F32)
    for ref in refs[1:-1]:
        summed = summed + ref[...].astype(F32)
    out[...] = summed.astype(BF16)


def on_device(
    tokens,
    tangent_tokens,
    log_decay,
    tangent_decay,
    w_inner,
    w_bmat,
    w_cmat,
    conv_inner,
    conv_bc,
    skip_gain,
    w_out,
):
    length, piece = tokens.shape
    model, width = w_inner.shape
    state_len = w_bmat.shape[1]
    channels = width + 2 * state_len
    heads = width // HEAD_DIM
    n_ctx, n_head = lax.axis_size("ctx"), lax.axis_size("head")
    chips = n_head // 2
    margin = conv_inner.shape[0] - 1
    shape = jax.ShapeDtypeStruct
    place = lax.axis_index("head")
    chip, core = place // 2, place % 2

    def along(values, distance):
        route = [
            (2 * i + j, 2 * ((i + distance) % chips) + j) for i in range(chips) for j in range(2)
        ]
        return lax.ppermute(values, "head", route)

    def swap(values):
        return lax.ppermute(values, "head", [(i, i ^ 1) for i in range(n_head)])

    def exchange(values):
        blocks = values.reshape(n_ctx, values.shape[0] // n_ctx, values.shape[1])
        return lax.all_to_all(blocks, "ctx", 0, 0).reshape(values.shape)

    first, second = tokens.T, tangent_tokens.T
    first_up, first_down, second_down = along(first, 1), along(first, -1), along(second, -1)
    pad = ((0, 16 - heads), (0, 0))
    dec = jnp.concatenate([jnp.pad(log_decay.T, pad), jnp.pad(tangent_decay.T, pad)], 0)
    table, columns, vec, tail = call(
        decay_body,
        [shape((80, length), F32), shape((length, 32), F32)]
        + [shape((8, width), F32), shape((8, 128), F32)],
        pinned=True,
        count=1,
        work=(10**8, 10**6),
    )(dec)
    first_up, table = lax.optimization_barrier((first_up, table))
    first_far = along(first_up, 1)
    later, first_far = lax.optimization_barrier((second, first_far))
    second_up = along(later, 1)
    second_far = along(second_down, -1)
    firsts = [first, first_up, first_down, first_far]
    seconds = [second, second_up, second_down, second_far]
    firsts = firsts + [swap(v) for v in firsts]
    seconds = seconds + [swap(v) for v in seconds]
    chip_of = [chip, chip - 1, chip + 1, chip + 2]
    order = jnp.stack(
        [(i + chips) % chips * 2 + core for i in chip_of]
        + [(i + chips) % chips * 2 + (1 - core) for i in chip_of]
    ).astype(jnp.int32)

    (edge,) = call(
        edge_body,
        [shape((16, piece), BF16)],
        [pltpu.VMEM((2, piece, 128), BF16)],
        held=(0, 1),
        count=2,
        work=(10**7, MIB // 4),
    )(first, second)
    edge = lax.ppermute(edge, "ctx", [(i, i + 1) for i in range(n_ctx - 1)])
    edge = lax.all_to_all(jnp.broadcast_to(edge[None], (n_head, *edge.shape)), "head", 0, 0)
    edge = edge.transpose(1, 0, 2).reshape(edge.shape[1], model)
    taps = jnp.concatenate([conv_inner, conv_bc], 1)
    (w_all,) = call(
        weight_body,
        [shape((model, channels), BF16)],
        near=(0, 1, 2),
        count=3,
        work=(10**6, 9 * MIB),
    )(w_inner, w_bmat, w_cmat)

    def scratch(spans):
        return [
            pltpu.VMEM((model, length), BF16),
            pltpu.VMEM((length + 8, channels), F32),
            pltpu.VMEM((length, channels), BF16),
            pltpu.VMEM((width, spans * SPAN), BF16),
            pltpu.SemaphoreType.DMA((8,)),
        ]

    work = (2 * channels * model * length, 12 * MIB)
    mix = shape((channels, length), BF16)
    state = shape((state_len, width), F32)
    mixed, gate, halo, state0, own = call(
        primal_body,
        [mix, shape((length, channels), F32), shape((16, channels), F32), state, state],
        scratch(1),
        near=(9,),
        held=tuple(range(1, 9)),
        pinned=(0, 3),
        count=14,
        smem=(0,),
        work=work,
        limit=20,
    )(order, *firsts, w_all, edge, taps, table, vec)
    mixed_dot, state0_dot, message = call(
        tangent_body,
        [mix, state, shape((2 * state_len, width + 128), BF16)],
        scratch(2),
        near=(9, 10, 15, 17),
        held=tuple(range(1, 9)),
        pinned=True,
        count=19,
        smem=(0,),
        work=work,
        limit=20,
    )(order, *seconds, w_all, halo, taps, table, vec, mixed, gate, state0, own, tail)

    arrived = exchange(message)
    gains = jnp.pad(skip_gain[None], ((0, 0), (0, 16 - heads)))
    wide = shape((width, length), F32)
    within, within_dot = call(
        within_body,
        [wide, wide],
        [pltpu.VMEM((SPAN, SPAN), F32)] * 2,
        pinned=True,
        count=5,
        work=(5 * 10**9, 8 * MIB),
        limit=BIG,
    )(mixed, mixed_dot, table, columns, gains)
    half = (lax.axis_index("ctx") % 2).astype(jnp.int32)[None]
    line = pltpu.VMEM((n_ctx, width // 2), F32)
    (leaving,) = call(
        scan_body,
        [shape((2 * state_len, width), BF16)],
        [pltpu.VMEM((2 * state_len, width), F32), line, line],
        near=(1,),
        count=2,
        smem=(0,),
        work=(10**8, MIB),
    )(half, arrived)
    entry = exchange(leaving)

    ring = [(chip + d) % chips for d in range(chips)]
    slices = jnp.stack([2 * i + j for i in ring for j in (core, 1 - core)]).astype(jnp.int32)
    side = shape((model // 2, width), BF16)
    keep, send = call(
        arrange_body, [side, side], near=(1,), count=2, smem=(0,), work=(10**6, 6 * MIB)
    )(slices, w_out.T)
    received = swap(send)
    values = shape((width, length), BF16)
    bc = width + state_len
    (inner,) = call(read_body, [values], count=6, work=(10**9, 4 * MIB), limit=BIG)(
        entry, mixed[bc:], within, table, vec, state0
    )
    inner, entry = lax.optimization_barrier((inner, entry))
    (inner_dot,) = call(read_dot_body, [values], count=8, work=(10**9, 6 * MIB), limit=BIG)(
        entry, mixed[bc:], mixed_dot[bc:], within_dot, table, vec, state0, state0_dot
    )
    term = shape((piece, length), BF16)
    product = call(
        product_body,
        [term] * chips,
        near=(0, 1, 2, 3),
        count=4,
        work=(2 * chips * piece * 2 * width * length, 6 * MIB),
    )

    def total(*terms):
        count = len(terms)
        body = call(total_body, [term], near=range(count), count=count, work=(10**6, 2 * MIB))
        return body(*terms)[0]

    def finish(values, way):
        terms = product(keep, received, values, swap(values))
        far = along(terms[2], way)
        near, back = (terms[1], terms[3]) if way == 1 else (terms[3], terms[1])
        back = along(back, -way)
        near = along(total(near, far), way)
        return total(terms[0], near, back).T

    return finish(inner, 1), finish(inner_dot, -1)


def solution(mesh):
    in_specs = (
        P("ctx", "head"),
        P("ctx", "head"),
        P("ctx", "head"),
        P("ctx", "head"),
        P(None, "head"),
        P(),
        P(),
        P(None, "head"),
        P(),
        P("head"),
        P("head", None),
    )
    out_specs = (P("ctx", "head"), P("ctx", "head"))
    return jax.shard_map(
        on_device, mesh=mesh, in_specs=in_specs, out_specs=out_specs, check_vma=False
    )
```

```python
import functools

import jax
import jax.numpy as jnp
from jax import lax
from jax.experimental import pallas as pl
from jax.experimental.pallas import tpu as pltpu
from jax.sharding import PartitionSpec as P

HEAD_DIM = 64
SPAN = 256
MIB = 1 << 20
BIG = 56
CHIPS = 4
AROUND = (0, CHIPS - 1, 1, 2)
BF16 = jnp.bfloat16
F32 = jnp.float32
HIGHEST = lax.Precision.HIGHEST

NN = (((1,), (0,)), ((), ()))
NT = (((1,), (1,)), ((), ()))
TN = (((0,), (0,)), ((), ()))


def mm(a, b, dims=NN, precision=None):
    return lax.dot_general(a, b, dims, precision=precision, preferred_element_type=F32)


def call(body, out, scratch=(), smem=(), near=(), held=(), pinned=(), count=0, work=(0, 0), limit=16):
    outs = list(out)
    n_out, n_scratch = len(outs), len(scratch)
    far = [i for i in range(count) if i not in smem and i not in held and i not in near]
    far_out = list(range(n_out)) if pinned is True else list(pinned)

    def kernel(*refs):
        ins, res = list(refs[:count]), list(refs[count : count + n_out])
        rest = refs[count + n_out :]
        own, rest = list(rest[:n_scratch]), list(rest[n_scratch:])
        copies, late = [], []
        for k, i in enumerate(far):
            copies.append(pltpu.make_async_copy(ins[i], rest[k], rest[-1].at[k]))
            ins[i] = rest[k]
        for k, i in enumerate(far_out, len(far)):
            late.append(pltpu.make_async_copy(rest[k], res[i], rest[-1].at[k]))
            res[i] = rest[k]
        for copy in copies:
            copy.start()
        if held:
            body(copies, *ins, *res, *own)
        else:
            for copy in copies:
                copy.wait()
            body(*ins, *res, *own)
        for copy in late:
            copy.start()
        for copy in late:
            copy.wait()

    def space(i):
        return pltpu.SMEM if i in smem else pltpu.VMEM if i in near else pltpu.HBM

    def run(*args):
        assert len(args) == count
        buffers = [pltpu.VMEM(args[i].shape, args[i].dtype) for i in far]
        buffers += [pltpu.VMEM(outs[i].shape, outs[i].dtype) for i in far_out]
        if buffers:
            buffers.append(pltpu.SemaphoreType.DMA((len(buffers),)))
        return pl.pallas_call(
            kernel,
            out_shape=[
                pltpu.HBM(v.shape, v.dtype) if i in far_out else v for i, v in enumerate(outs)
            ],
            in_specs=[pl.BlockSpec(memory_space=space(i)) for i in range(count)],
            out_specs=[
                pl.BlockSpec(memory_space=pltpu.HBM if i in far_out else pltpu.VMEM)
                for i in range(n_out)
            ],
            scratch_shapes=list(scratch) + buffers,
            cost_estimate=pl.CostEstimate(
                flops=work[0], bytes_accessed=work[1], transcendentals=0
            ),
            compiler_params=pltpu.CompilerParams(vmem_limit_bytes=limit * MIB),
        )(*args)

    return run


def spread(rows, width):
    head = lax.broadcasted_iota(jnp.int32, (rows, width), 0)
    lane = lax.broadcasted_iota(jnp.int32, (rows, width), 1)
    return jnp.where(lane // HEAD_DIM == head, 1.0, 0.0).astype(F32)


CUM, CUM_DOT, REM, REM_DOT, CUM_EXP = 0, 16, 32, 48, 64


def decay_body(dec, table, columns, vec, tail):
    s = lax.broadcasted_iota(jnp.int32, (SPAN, SPAN), 0)
    t = lax.broadcasted_iota(jnp.int32, (SPAN, SPAN), 1)
    upper = jnp.where(s <= t, 1.0, 0.0).astype(F32)
    lower = jnp.where(t <= s, 1.0, 0.0).astype(F32)
    ends = []
    for b in range(dec.shape[1] // SPAN):
        lanes = slice(b * SPAN, (b + 1) * SPAN)
        both = dec[:, lanes]
        c = mm(both, upper, NN, HIGHEST)
        c_t = mm(lower, both, NT, HIGHEST)
        p, d = c[:16], c[16:]
        table[CUM : CUM + 16, lanes] = p
        table[CUM_DOT : CUM_DOT + 16, lanes] = d
        table[CUM_EXP : CUM_EXP + 16, lanes] = jnp.exp(p)
        r = jnp.exp(p[:, SPAN - 1 :] - p)
        table[REM : REM + 16, lanes] = r
        table[REM_DOT : REM_DOT + 16, lanes] = r * (d[:, SPAN - 1 :] - d)
        columns[lanes, :] = c_t
        ends.append(c_t[SPAN - 1 :, :])
    rows = jnp.concatenate(
        [ends[0][:, :16], ends[0][:, 16:], ends[1][:, :16], ends[1][:, 16:]]
        + [jnp.zeros((4, 16), F32)],
        0,
    )
    wide = mm(rows, spread(16, vec.shape[1]), NN, HIGHEST)
    row = lax.broadcasted_iota(jnp.int32, wide.shape, 0)
    vec[...] = jnp.where((row == 0) | (row == 2), jnp.exp(wide), wide)
    rest = ends[0] + ends[1]
    tail[...] = jnp.zeros(tail.shape, F32)
    for i in range(3):
        term = rest.astype(BF16).astype(F32)
        tail[i : i + 1, 0:32] = term
        rest = rest - term


def group(place, distance, other):
    chip, core = place[0] // 2, place[0] % 2
    return (chip + distance) % CHIPS * 2 + (1 - core if other else core)


def gather(place, pieces, full, sems):
    rows = pieces[0].shape[0]
    arriving = []
    for i, piece in enumerate(pieces):
        at = group(place, AROUND[i % 4], i >= 4) * rows
        here = full.at[pl.ds(pl.multiple_of(at, rows), rows), :]
        arriving.append(pltpu.make_async_copy(piece, here, sems.at[i]))
    for copy in arriving:
        copy.start()
    return arriving


CHUNK = 64


def convolve(ext, taps, store):
    count = taps.shape[0]
    for c in range(taps.shape[1] // 128):
        lanes = slice(c * 128, (c + 1) * 128)
        kernel = [jnp.broadcast_to(taps[k : k + 1, lanes], (CHUNK, 128)) for k in range(count)]
        for r in range(0, SPAN, CHUNK):
            summed = None
            for k in range(count):
                at = r + 9 - count + k
                term = kernel[k] * ext[at : at + CHUNK, lanes]
                summed = term if summed is None else summed + term
            store(slice(r, r + CHUNK), lanes, summed)


def turn(rows):
    s = lax.broadcasted_iota(jnp.int32, (SPAN, SPAN), 0)
    t = lax.broadcasted_iota(jnp.int32, (SPAN, SPAN), 1)
    return mm(rows, jnp.where(s == t, 1.0, 0.0).astype(BF16), TN).astype(BF16)


def to_owners(values):
    n, width = values.shape
    halves = [values[:, : width // 2], values[:, width // 2 :]]
    stacked = jnp.stack([v.reshape(n // 8, 8, width // 2) for v in halves], 1)
    return stacked.reshape(2 * n, width // 2)


def from_owners(values):
    n, width = values.shape
    split = values.reshape(n // 16, 2, 8, width)
    return jnp.concatenate([split[:, i].reshape(n // 2, width) for i in range(2)], 1)


def project(place, pieces, weights, out, full, w_all, total, sems):
    arriving = gather(place, pieces, full, sems)
    half = w_all.shape[0] // 2
    coming = []
    for part in range(2):
        rows = slice(part * half, (part + 1) * half)
        at = 0
        for i, weight in enumerate(weights):
            columns = slice(at, at + weight.shape[1])
            at = columns.stop
            copy = pltpu.make_async_copy(
                weight.at[rows, :], w_all.at[rows, columns], sems.at[8 + 3 * part + i]
            )
            copy.start()
            coming.append(copy)
    for copy in [*arriving, *coming[:3]]:
        copy.wait()
    total[...] = mm(full[:half, :], w_all[:half, :], TN)
    for copy in coming[3:]:
        copy.wait()
    out[...] = (total[...] + mm(full[half:, :], w_all[half:, :], TN)).astype(BF16)


def primal_body(copies, place, *refs):
    project(place, refs[:8], refs[8:11], *refs[11:])


def tangent_body(copies, place, *refs):
    first, projected, edge, full, w_all, total, last, sems = refs[11:]
    length = full.shape[1]
    ending = pltpu.make_async_copy(first.at[length - 16 :, :], last, sems.at[14])
    ending.start()
    project(place, refs[:8], refs[8:11], projected, full, w_all, total, sems)
    ending.wait()
    ends = [last[...].astype(F32)[8:], projected[length - 16 :, :].astype(F32)[8:]]
    edge[...] = jnp.concatenate(ends, 0).astype(BF16)


def block_body(b, projected, projected_dot, before, taps, table, vec, tail, *refs):
    if b == 0:
        state1, state1_dot, mixed, mixed_dot, state, state_dot, message = refs[:7]
        refs = refs[7:]
    else:
        mixed, mixed_dot, state, state_dot = refs[:4]
        refs = refs[4:]
    ext, ext_dot, gate, rows, rows_dot, scaled = refs
    at = slice(b * SPAN, (b + 1) * SPAN)
    for i, (source, out) in enumerate(((projected, ext), (projected_dot, ext_dot))):
        ahead = before[...].astype(F32)[8 * i : 8 * i + 8]
        if b > 0:
            ahead = source[b * SPAN - 16 : b * SPAN, :].astype(F32)[8:]
        out[0:8, :] = ahead
        out[8:, :] = source[at, :].astype(F32)

    def store(where, lanes, v):
        sig = 1.0 / (1.0 + jnp.exp(-v))
        rows[where, lanes] = (v * sig).astype(BF16)
        gate[where, lanes] = sig * (1.0 + v * (1.0 - sig))

    def store_dot(where, lanes, v):
        rows_dot[where, lanes] = (gate[where, lanes] * v).astype(BF16)

    convolve(ext, taps, store)
    mixed[...] = turn(rows[...])
    convolve(ext_dot, taps, store_dot)
    mixed_dot[...] = turn(rows_dot[...])
    width = vec.shape[1]
    for h in range(width // HEAD_DIM):
        here = slice(h * HEAD_DIM, (h + 1) * HEAD_DIM)
        value = mixed[here, :].astype(F32)
        r = table[REM + h : REM + h + 1, at]
        scaled[here, SPAN:] = (value * r).astype(BF16)
        scaled[here, :SPAN] = (
            mixed_dot[here, :].astype(F32) * r + value * table[REM_DOT + h : REM_DOT + h + 1, at]
        ).astype(BF16)
    writer = mixed[width : width + 128, :]
    writer_dot = mixed_dot[width : width + 128, :]
    own = mm(writer, scaled[:, SPAN:], NT)
    own_dot = mm(writer, scaled[:, :SPAN], NT) + mm(writer_dot, scaled[:, SPAN:], NT)
    state[...] = own
    state_dot[...] = own_dot
    if b == 0:
        own_dot = vec[2:3, :] * (own_dot + vec[3:4, :] * own) + state1_dot[...]
        own = vec[2:3, :] * own + state1[...]
        message[:, : width // 2] = to_owners(own).astype(BF16)
        message[:, width // 2 : width] = to_owners(own_dot).astype(BF16)
        both = jnp.concatenate([tail[...], tail[...]], 0).astype(BF16)
        for j in range(message.shape[0] // 16):
            message[16 * j : 16 * j + 16, width:] = both


def within_body(first, second, first_dot, second_dot, table, columns, gain, within, within_dot, sc, scd):
    width = within.shape[0]
    state = (first.shape[0] - width) // 2
    s = lax.broadcasted_iota(jnp.int32, (SPAN, SPAN), 0)
    t = lax.broadcasted_iota(jnp.int32, (SPAN, SPAN), 1)
    causal = s <= t
    for b in range(2):
        lanes = slice(b * SPAN, (b + 1) * SPAN)
        mixed, mixed_dot = ((first, first_dot), (second, second_dot))[b]
        writer, reader = mixed[width : width + state, :], mixed[width + state :, :]
        writer_dot, reader_dot = mixed_dot[width : width + state, :], mixed_dot[width + state :, :]
        sc[...] = mm(writer, reader, TN)
        scd[...] = mm(writer_dot, reader, TN) + mm(writer, reader_dot, TN)
        for h in range(width // HEAD_DIM):
            rows = slice(h * HEAD_DIM, (h + 1) * HEAD_DIM)
            diff = table[CUM + h : CUM + h + 1, lanes] - columns[lanes, h : h + 1]
            diff_dot = (
                table[CUM_DOT + h : CUM_DOT + h + 1, lanes] - columns[lanes, 16 + h : 17 + h]
            )
            weight = jnp.exp(jnp.where(causal, diff, -jnp.inf))
            mix = (weight * sc[...]).astype(BF16)
            mix_dot = (weight * (scd[...] + diff_dot * sc[...])).astype(BF16)
            value, value_dot = mixed[rows, :], mixed_dot[rows, :]
            both = mm(jnp.concatenate([value, value_dot], 0), mix)
            other = mm(value, mix_dot)
            skip = gain[0:1, h : h + 1]
            within[rows, lanes] = both[:HEAD_DIM] + skip * value.astype(F32)
            within_dot[rows, lanes] = (both[HEAD_DIM:] + other) + skip * value_dot.astype(F32)


def unpack(half, width, which):
    lane = lax.broadcasted_iota(jnp.int32, (128, width), 0)
    head = lax.broadcasted_iota(jnp.int32, (128, width), 1) // HEAD_DIM + half * (width // HEAD_DIM)
    return jnp.where(lane == head + 16 * which, 1.0, 0.0).astype(BF16)


def scan_body(half, arrived, leaving, states, retain, slope):
    rows, whole = 8, leaving.shape[1]
    width = whole // 2
    steps = arrived.shape[0] // rows
    tails = arrived[:, whole:]
    for which, out in ((0, retain), (1, slope)):
        terms = mm(tails, unpack(half[0], width, which)).reshape(steps, rows, width)
        out[...] = (terms[:, 0] + terms[:, 1]) + terms[:, 2]
    retain[...] = jnp.exp(retain[...])
    states[...] = arrived[:, :whole].astype(F32)
    state = jnp.zeros((rows, width), F32)
    state_dot = jnp.zeros((rows, width), F32)
    for j in range(steps):
        own = slice(j * rows, (j + 1) * rows)
        arriving, arriving_dot = states[own, :width], states[own, width:]
        states[own, :width] = state
        states[own, width:] = state_dot
        r = retain[j : j + 1, :]
        state_dot = r * (state_dot + slope[j : j + 1, :] * state) + arriving_dot
        state = r * state + arriving
    leaving[...] = states[...].astype(BF16)


def arrange_body(place, w_t, keep, send):
    rows = w_t.shape[0] // (2 * CHIPS)
    for d in range(CHIPS):
        own = slice(d * rows, (d + 1) * rows)
        for other, out in ((False, keep), (True, send)):
            at = pl.multiple_of(group(place, d, other) * rows, rows)
            out[own, :] = w_t[pl.ds(at, rows), :]


def own_body(keep, own, out):
    for b in range(own.shape[1] // SPAN):
        lanes = slice(b * SPAN, (b + 1) * SPAN)
        out[:, lanes] = mm(keep[...], own[:, lanes])


def product_body(begun, received, other, *outs):
    rows = outs[0].shape[0]
    for b in range(other.shape[1] // SPAN):
        lanes = slice(b * SPAN, (b + 1) * SPAN)
        result = begun[:, lanes] + mm(received[...], other[:, lanes])
        for d, out in enumerate(outs):
            out[:, lanes] = result[d * rows : (d + 1) * rows].astype(BF16)


def read_body(
    copies, arrived, first, second, first_dot, second_dot, within, within_dot, table, vec, s0, s0_dot,
    inner, inner_dot, readers, readers_dot, sems,
):
    n = readers.shape[0]
    reading = []
    for i, (source, out) in enumerate(
        ((first, readers), (second, readers), (first_dot, readers_dot), (second_dot, readers_dot))
    ):
        lanes = slice((i % 2) * SPAN, (i % 2 + 1) * SPAN)
        reading.append(
            pltpu.make_async_copy(
                source.at[source.shape[0] - n :, :], out.at[:, lanes], sems.at[i]
            )
        )
    for copy in reading:
        copy.start()
    for copy in [*copies, *reading]:
        copy.wait()
    width = within.shape[0]
    entry = from_owners(arrived[:, : width // 2].astype(F32))
    entry_dot = from_owners(arrived[:, width // 2 :].astype(F32))
    for b in range(2):
        lanes = slice(b * SPAN, (b + 1) * SPAN)
        reader, reader_dot = readers[:, lanes], readers_dot[:, lanes]
        rounded = entry.astype(BF16)
        read = mm(rounded, reader, TN)
        read_dot = mm(rounded, reader_dot, TN) + mm(entry_dot.astype(BF16), reader, TN)
        for h in range(width // HEAD_DIM):
            rows = slice(h * HEAD_DIM, (h + 1) * HEAD_DIM)
            e = table[CUM_EXP + h : CUM_EXP + h + 1, lanes]
            d = table[CUM_DOT + h : CUM_DOT + h + 1, lanes]
            inner[rows, lanes] = (within[rows, lanes] + e * read[rows]).astype(BF16)
            inner_dot[rows, lanes] = (
                within_dot[rows, lanes] + e * (read_dot[rows] + d * read[rows])
            ).astype(BF16)
        if b == 0:
            retain, slope = vec[0:1, :], vec[1:2, :]
            entry_dot = retain * (entry_dot + slope * entry) + s0_dot[...]
            entry = retain * entry + s0[...]


def total_body(*refs):
    out = refs[-1]
    summed = refs[0][...].astype(F32)
    for ref in refs[1:-1]:
        summed = summed + ref[...].astype(F32)
    out[...] = summed.astype(BF16)


def on_device(
    tokens,
    tangent_tokens,
    log_decay,
    tangent_decay,
    w_inner,
    w_bmat,
    w_cmat,
    conv_inner,
    conv_bc,
    skip_gain,
    w_out,
):
    length, piece = tokens.shape
    model, width = w_inner.shape
    state_len = w_bmat.shape[1]
    channels = width + 2 * state_len
    heads = width // HEAD_DIM
    n_ctx, n_head = lax.axis_size("ctx"), lax.axis_size("head")
    chips = n_head // 2
    margin = conv_inner.shape[0] - 1
    shape = jax.ShapeDtypeStruct
    place = lax.axis_index("head")

    def along(values, distance):
        route = [
            (2 * i + j, 2 * ((i + distance) % chips) + j) for i in range(chips) for j in range(2)
        ]
        return lax.ppermute(values, "head", route)

    def swap(values):
        return lax.ppermute(values, "head", [(i, i ^ 1) for i in range(n_head)])

    def exchange(values):
        blocks = values.reshape(n_ctx, values.shape[0] // n_ctx, values.shape[1])
        return lax.all_to_all(blocks, "ctx", 0, 0).reshape(values.shape)

    first, second = tokens.T, tangent_tokens.T
    first_up, first_down = along(first, 1), along(first, -1)

    second_down = along(second, -1)
    pad = ((0, 16 - heads), (0, 0))
    dec = jnp.concatenate([jnp.pad(log_decay.T, pad), jnp.pad(tangent_decay.T, pad)], 0)
    table, columns, vec, tail = call(
        decay_body,
        [shape((80, length), F32), shape((length, 32), F32)]
        + [shape((8, width), F32), shape((8, 128), F32)],
        pinned=True,
        count=1,
        work=(10**8, 10**6),
    )(dec)
    first_up, table = lax.optimization_barrier((first_up, table))
    first_far = along(first_up, 1)
    later, first_far = lax.optimization_barrier((second, first_far))
    second_up = along(later, 1)
    second_far = along(second_down, -1)
    firsts = [first, first_up, first_down, first_far]
    firsts = firsts + [swap(v) for v in firsts]
    here = place[None]
    taps = jnp.concatenate([conv_inner, conv_bc], 1)

    full = [pltpu.VMEM((model, length), BF16), pltpu.VMEM((model, channels), BF16)]
    full += [pltpu.VMEM((length, channels), F32)]
    work = (2 * channels * model * length, 12 * MIB)
    tokens_by = shape((length, channels), BF16)
    (projected,) = call(
        primal_body,
        [tokens_by],
        [*full, pltpu.SemaphoreType.DMA((14,))],
        held=tuple(range(1, 12)),
        count=12,
        smem=(0,),
        work=work,
        limit=BIG,
    )(here, *firsts, w_inner, w_bmat, w_cmat)
    second_up, second_far, projected = lax.optimization_barrier(
        (second_up, second_far, projected)
    )
    seconds = [second, second_up, second_down, second_far]
    seconds = seconds + [swap(second), swap(second_up), swap(second_down), swap(second_far)]
    projected_dot, edge = call(
        tangent_body,
        [tokens_by, shape((16, channels), BF16)],
        [*full, pltpu.VMEM((16, channels), BF16), pltpu.SemaphoreType.DMA((15,))],
        held=tuple(range(1, 13)),
        count=13,
        smem=(0,),
        work=work,
        limit=BIG,
    )(here, *seconds, w_inner, w_bmat, w_cmat, projected)
    before = lax.ppermute(edge, "ctx", [(i, i + 1) for i in range(n_ctx - 1)])
    mix = shape((channels, SPAN), BF16)
    state = shape((state_len, width), F32)

    def block(b, out, before, *more):
        args = (projected, projected_dot, before, taps, table, vec, tail, *more)
        return call(
            functools.partial(block_body, b),
            [mix, mix, state, state, *out],
            [pltpu.VMEM((SPAN + 8, channels), F32)] * 2
            + [pltpu.VMEM((SPAN, channels), F32)]
            + [pltpu.VMEM((SPAN, channels), BF16)] * 2
            + [pltpu.VMEM((width, 2 * SPAN), BF16)],
            near=(0, 1, 2, 7, 8),
            pinned=(0, 1, 2, 3, 4) if out else (0, 1),
            count=len(args),
            work=(10**9, 8 * MIB),
            limit=20,
        )(*args)

    mixed1, mixed1_dot, state1, state1_dot = block(1, [], edge)
    mixed0, mixed0_dot, state0, state0_dot, message = block(
        0, [shape((2 * state_len, width + 128), BF16)], before, state1, state1_dot
    )

    arrived = exchange(message)
    gains = jnp.pad(skip_gain[None], ((0, 0), (0, 16 - heads)))
    wide = shape((width, length), F32)
    within, within_dot = call(
        within_body,
        [wide, wide],
        [pltpu.VMEM((SPAN, SPAN), F32)] * 2,
        pinned=True,
        count=7,
        work=(5 * 10**9, 8 * MIB),
        limit=BIG,
    )(mixed0, mixed1, mixed0_dot, mixed1_dot, table, columns, gains)
    half = (lax.axis_index("ctx") % 2).astype(jnp.int32)[None]
    line = pltpu.VMEM((n_ctx, width // 2), F32)
    (leaving,) = call(
        scan_body,
        [shape((2 * state_len, width), BF16)],
        [pltpu.VMEM((2 * state_len, width), F32), line, line],
        near=(1,),
        count=2,
        smem=(0,),
        work=(10**8, MIB),
    )(half, arrived)
    entry = exchange(leaving)

    side = shape((model // 2, width), BF16)
    keep, send = call(
        arrange_body, [side, side], near=(1,), count=2, smem=(0,), work=(10**6, 6 * MIB)
    )(here, w_out.T)
    received = swap(send)
    values = shape((width, length), BF16)
    reader = pltpu.VMEM((state_len, length), BF16)
    inner, inner_dot = call(
        read_body,
        [values, values],
        [reader, reader, pltpu.SemaphoreType.DMA((4,))],
        near=(0,),
        held=(1, 2, 3, 4),
        count=11,
        work=(10**9, 6 * MIB),
        limit=BIG,
    )(
        entry, mixed0, mixed1, mixed0_dot, mixed1_dot, within, within_dot, table, vec, state0,
        state0_dot,
    )
    term = shape((piece, length), BF16)
    work = (2 * chips * piece * width * length, 4 * MIB)
    begin = call(
        own_body, [shape((chips * piece, length), F32)], near=(0, 1), count=2, work=work
    )
    product = call(product_body, [term] * chips, near=(0, 1, 2), count=3, work=work)

    def total(*terms):
        count = len(terms)
        body = call(total_body, [term], near=range(count), count=count, work=(10**6, 2 * MIB))
        return body(*terms)[0]

    def finish(begun, other, way):
        terms = product(begun, received, other)
        far = along(terms[2], way)
        near, back = (terms[1], terms[3]) if way == 1 else (terms[3], terms[1])
        back = along(back, -way)
        near = along(total(near, far), way)
        return total(terms[0], near, back).T

    other, other_dot = swap(inner), swap(inner_dot)
    begun, begun_dot = begin(keep, inner)[0], begin(keep, inner_dot)[0]
    return finish(begun, other, 1), finish(begun_dot, other_dot, -1)


def solution(mesh):
    in_specs = (
        P("ctx", "head"),
        P("ctx", "head"),
        P("ctx", "head"),
        P("ctx", "head"),
        P(None, "head"),
        P(),
        P(),
        P(None, "head"),
        P(),
        P("head"),
        P("head", None),
    )
    out_specs = (P("ctx", "head"), P("ctx", "head"))
    return jax.shard_map(
        on_device, mesh=mesh, in_specs=in_specs, out_specs=out_specs, check_vma=False
    )
```

```python
import functools

import jax
import jax.numpy as jnp
from jax import lax
from jax.experimental import pallas as pl
from jax.experimental.pallas import tpu as pltpu
from jax.sharding import PartitionSpec as P

HEAD_DIM = 64
SPAN = 256
MIB = 1 << 20
BIG = 24
CHIPS = 4
AROUND = (0, CHIPS - 1, 1, 2)
BF16 = jnp.bfloat16
F32 = jnp.float32
HIGHEST = lax.Precision.HIGHEST

NN = (((1,), (0,)), ((), ()))
NT = (((1,), (1,)), ((), ()))
TN = (((0,), (0,)), ((), ()))


def mm(a, b, dims=NN, precision=None):
    return lax.dot_general(a, b, dims, precision=precision, preferred_element_type=F32)


def call(body, out, scratch=(), smem=(), near=(), held=(), loose=(), pinned=(), count=0, work=(0, 0), limit=16):
    outs = list(out)
    n_out, n_scratch = len(outs), len(scratch)
    far = [i for i in range(count) if i not in smem and i not in held and i not in near]
    far_out = list(range(n_out)) if pinned is True else list(pinned)

    def kernel(*refs):
        ins, res = list(refs[:count]), list(refs[count : count + n_out])
        rest = refs[count + n_out :]
        own, rest = list(rest[:n_scratch]), list(rest[n_scratch:])
        copies, late = [], []
        for k, i in enumerate(far):
            copies.append(pltpu.make_async_copy(ins[i], rest[k], rest[-1].at[k]))
            ins[i] = rest[k]
        for k, i in enumerate(far_out, len(far)):
            late.append(pltpu.make_async_copy(rest[k], res[i], rest[-1].at[k]))
            res[i] = rest[k]
        for copy in copies:
            copy.start()
        if held:
            body(copies, *ins, *res, *own)
        else:
            for copy in copies:
                copy.wait()
            body(*ins, *res, *own)
        for copy in late:
            copy.start()
        for copy in late:
            copy.wait()

    def space(i):
        if i in smem:
            return pltpu.SMEM
        return pltpu.VMEM if i in near else pl.ANY if i in loose else pltpu.HBM

    def run(*args):
        assert len(args) == count
        buffers = [pltpu.VMEM(args[i].shape, args[i].dtype) for i in far]
        args = [
            pltpu.with_memory_space_constraint(v, pltpu.HBM) if space(i) is pltpu.HBM else v
            for i, v in enumerate(args)
        ]
        buffers += [pltpu.VMEM(outs[i].shape, outs[i].dtype) for i in far_out]
        if buffers:
            buffers.append(pltpu.SemaphoreType.DMA((len(buffers),)))
        return pl.pallas_call(
            kernel,
            out_shape=[
                pltpu.HBM(v.shape, v.dtype) if i in far_out else v for i, v in enumerate(outs)
            ],
            in_specs=[pl.BlockSpec(memory_space=space(i)) for i in range(count)],
            out_specs=[
                pl.BlockSpec(memory_space=pltpu.HBM if i in far_out else pltpu.VMEM)
                for i in range(n_out)
            ],
            scratch_shapes=list(scratch) + buffers,
            cost_estimate=pl.CostEstimate(
                flops=work[0], bytes_accessed=work[1], transcendentals=0
            ),
            compiler_params=pltpu.CompilerParams(vmem_limit_bytes=limit * MIB),
        )(*args)

    return run


def spread(rows, width):
    head = lax.broadcasted_iota(jnp.int32, (rows, width), 0)
    lane = lax.broadcasted_iota(jnp.int32, (rows, width), 1)
    return jnp.where(lane // HEAD_DIM == head, 1.0, 0.0).astype(F32)


CUM, CUM_DOT, REM, REM_DOT, CUM_EXP = 0, 16, 32, 48, 64


def decay_body(dec, table, columns, vec, tail):
    s = lax.broadcasted_iota(jnp.int32, (SPAN, SPAN), 0)
    t = lax.broadcasted_iota(jnp.int32, (SPAN, SPAN), 1)
    upper = jnp.where(s <= t, 1.0, 0.0).astype(F32)
    lower = jnp.where(t <= s, 1.0, 0.0).astype(F32)
    ends = []
    for b in range(dec.shape[1] // SPAN):
        lanes = slice(b * SPAN, (b + 1) * SPAN)
        both = dec[:, lanes]
        c = mm(both, upper, NN, HIGHEST)
        c_t = mm(lower, both, NT, HIGHEST)
        p, d = c[:16], c[16:]
        table[CUM : CUM + 16, lanes] = p
        table[CUM_DOT : CUM_DOT + 16, lanes] = d
        table[CUM_EXP : CUM_EXP + 16, lanes] = jnp.exp(p)
        r = jnp.exp(p[:, SPAN - 1 :] - p)
        table[REM : REM + 16, lanes] = r
        table[REM_DOT : REM_DOT + 16, lanes] = r * (d[:, SPAN - 1 :] - d)
        columns[lanes, :] = c_t
        ends.append(c_t[SPAN - 1 :, :])
    rows = jnp.concatenate(
        [ends[0][:, :16], ends[0][:, 16:], ends[1][:, :16], ends[1][:, 16:]]
        + [jnp.zeros((4, 16), F32)],
        0,
    )
    wide = mm(rows, spread(16, vec.shape[1]), NN, HIGHEST)
    row = lax.broadcasted_iota(jnp.int32, wide.shape, 0)
    vec[...] = jnp.where((row == 0) | (row == 2), jnp.exp(wide), wide)
    rest = ends[0] + ends[1]
    tail[...] = jnp.zeros(tail.shape, F32)
    for i in range(3):
        term = rest.astype(BF16).astype(F32)
        tail[i : i + 1, 0:32] = term
        rest = rest - term


def group(place, distance, other):
    chip, core = place[0] // 2, place[0] % 2
    return (chip + distance) % CHIPS * 2 + (1 - core if other else core)


def gather(place, pieces, full, sems):
    rows = pieces[0].shape[0]
    arriving = []
    for i, piece in enumerate(pieces):
        at = group(place, AROUND[i % 4], i >= 4) * rows
        here = full.at[pl.ds(pl.multiple_of(at, rows), rows), :]
        arriving.append(pltpu.make_async_copy(piece, here, sems.at[i]))
    for copy in arriving:
        copy.start()
    return arriving


CHUNK = 64


def convolve(ext, taps, store):
    count = taps.shape[0]
    for c in range(taps.shape[1] // 128):
        lanes = slice(c * 128, (c + 1) * 128)
        kernel = [jnp.broadcast_to(taps[k : k + 1, lanes], (CHUNK, 128)) for k in range(count)]
        for r in range(0, SPAN, CHUNK):
            summed = None
            for k in range(count):
                at = r + 9 - count + k
                term = kernel[k] * ext[at : at + CHUNK, lanes]
                summed = term if summed is None else summed + term
            store(slice(r, r + CHUNK), lanes, summed)


def turn(rows):
    s = lax.broadcasted_iota(jnp.int32, (SPAN, SPAN), 0)
    t = lax.broadcasted_iota(jnp.int32, (SPAN, SPAN), 1)
    return mm(rows, jnp.where(s == t, 1.0, 0.0).astype(BF16), TN).astype(BF16)


def to_owners(values):
    n, width = values.shape
    halves = [values[:, : width // 2], values[:, width // 2 :]]
    stacked = jnp.stack([v.reshape(n // 8, 8, width // 2) for v in halves], 1)
    return stacked.reshape(2 * n, width // 2)


def from_owners(values):
    n, width = values.shape
    split = values.reshape(n // 16, 2, 8, width)
    return jnp.concatenate([split[:, i].reshape(n // 2, width) for i in range(2)], 1)


def project(place, pieces, weights, out, full, w_all, total, sems):
    arriving = gather(place, pieces, full, sems)
    half = w_all.shape[0] // 2
    coming = []
    for part in range(2):
        rows = slice(part * half, (part + 1) * half)
        at = 0
        for i, weight in enumerate(weights):
            columns = slice(at, at + weight.shape[1])
            at = columns.stop
            copy = pltpu.make_async_copy(
                weight.at[rows, :], w_all.at[rows, columns], sems.at[8 + 3 * part + i]
            )
            copy.start()
            coming.append(copy)
    for copy in [*arriving, *coming[:3]]:
        copy.wait()
    total[...] = mm(full[:half, :], w_all[:half, :], TN)
    for copy in coming[3:]:
        copy.wait()
    out[...] = (total[...] + mm(full[half:, :], w_all[half:, :], TN)).astype(BF16)


def primal_body(copies, place, *refs):
    project(place, refs[:8], refs[8:11], *refs[11:])


def tangent_body(copies, place, *refs):
    first, projected, edge, full, w_all, total, last, sems = refs[11:]
    length = full.shape[1]
    ending = pltpu.make_async_copy(first.at[length - 16 :, :], last, sems.at[14])
    ending.start()
    project(place, refs[:8], refs[8:11], projected, full, w_all, total, sems)
    ending.wait()
    ends = [last[...].astype(F32)[8:], projected[length - 16 :, :].astype(F32)[8:]]
    edge[...] = jnp.concatenate(ends, 0).astype(BF16)


def block_body(b, projected, projected_dot, taps, table, vec, tail, *refs):
    if b == 0:
        before, state1, state1_dot, mixed, mixed_dot, state, state_dot, message = refs[:8]
        refs = refs[8:]
    else:
        mixed, mixed_dot, state, state_dot = refs[:4]
        refs = refs[4:]
    ext, ext_dot, gate, rows, rows_dot, scaled = refs
    at = slice(b * SPAN, (b + 1) * SPAN)
    for i, (source, out) in enumerate(((projected, ext), (projected_dot, ext_dot))):
        if b > 0:
            ahead = source[b * SPAN - 16 : b * SPAN, :].astype(F32)[8:]
        else:
            ahead = before[...].astype(F32)[8 * i : 8 * i + 8]
        out[0:8, :] = ahead
        out[8:, :] = source[at, :].astype(F32)

    def store(where, lanes, v):
        sig = 0.5 + 0.5 * jnp.tanh(0.5 * v)
        rows[where, lanes] = (v * sig).astype(BF16)
        gate[where, lanes] = sig * (1.0 + v * (1.0 - sig))

    def store_dot(where, lanes, v):
        rows_dot[where, lanes] = (gate[where, lanes] * v).astype(BF16)

    convolve(ext, taps, store)
    mixed[...] = turn(rows[...])
    convolve(ext_dot, taps, store_dot)
    mixed_dot[...] = turn(rows_dot[...])
    width = vec.shape[1]
    for h in range(width // HEAD_DIM):
        here = slice(h * HEAD_DIM, (h + 1) * HEAD_DIM)
        value = mixed[here, :].astype(F32)
        r = table[REM + h : REM + h + 1, at]
        scaled[here, SPAN:] = (value * r).astype(BF16)
        scaled[here, :SPAN] = (
            mixed_dot[here, :].astype(F32) * r + value * table[REM_DOT + h : REM_DOT + h + 1, at]
        ).astype(BF16)
    writer = mixed[width : width + 128, :]
    writer_dot = mixed_dot[width : width + 128, :]
    own = mm(writer, scaled[:, SPAN:], NT)
    own_dot = mm(jnp.concatenate([writer, writer_dot], 1), scaled[...], NT)
    state[...] = own
    state_dot[...] = own_dot
    if b == 0:
        own_dot = vec[2:3, :] * (own_dot + vec[3:4, :] * own) + state1_dot[...]
        own = vec[2:3, :] * own + state1[...]
        message[:, : width // 2] = to_owners(own).astype(BF16)
        message[:, width // 2 : width] = to_owners(own_dot).astype(BF16)
        both = jnp.concatenate([tail[...], tail[...]], 0).astype(BF16)
        for j in range(message.shape[0] // 16):
            message[16 * j : 16 * j + 16, width:] = both


def within_body(first, second, first_dot, second_dot, table, columns, gain, within, within_dot, sc, scd):
    width = within.shape[0]
    state = (first.shape[0] - width) // 2
    s = lax.broadcasted_iota(jnp.int32, (SPAN, SPAN), 0)
    t = lax.broadcasted_iota(jnp.int32, (SPAN, SPAN), 1)
    causal = s <= t
    for b in range(2):
        lanes = slice(b * SPAN, (b + 1) * SPAN)
        mixed, mixed_dot = ((first, first_dot), (second, second_dot))[b]
        writer, reader = mixed[width : width + state, :], mixed[width + state :, :]
        writer_dot, reader_dot = mixed_dot[width : width + state, :], mixed_dot[width + state :, :]
        sc[...] = mm(writer, reader, TN)
        scd[...] = mm(jnp.concatenate([writer_dot, writer], 0), jnp.concatenate([reader, reader_dot], 0), TN)
        for h in range(width // HEAD_DIM):
            rows = slice(h * HEAD_DIM, (h + 1) * HEAD_DIM)
            diff = table[CUM + h : CUM + h + 1, lanes] - columns[lanes, h : h + 1]
            diff_dot = (
                table[CUM_DOT + h : CUM_DOT + h + 1, lanes] - columns[lanes, 16 + h : 17 + h]
            )
            weight = jnp.exp(jnp.where(causal, diff, -jnp.inf))
            mix = (weight * sc[...]).astype(BF16)
            mix_dot = (weight * (scd[...] + diff_dot * sc[...])).astype(BF16)
            value, value_dot = mixed[rows, :], mixed_dot[rows, :]
            both = mm(jnp.concatenate([value, value_dot], 0), mix)
            other = mm(value, mix_dot)
            skip = gain[0:1, h : h + 1]
            within[rows, lanes] = both[:HEAD_DIM] + skip * value.astype(F32)
            within_dot[rows, lanes] = (both[HEAD_DIM:] + other) + skip * value_dot.astype(F32)


def unpack(half, width, which):
    lane = lax.broadcasted_iota(jnp.int32, (128, width), 0)
    head = lax.broadcasted_iota(jnp.int32, (128, width), 1) // HEAD_DIM + half * (width // HEAD_DIM)
    return jnp.where(lane == head + 16 * which, 1.0, 0.0).astype(BF16)


def scan_body(half, arrived, leaving, states, retain, slope):
    rows, whole = 8, leaving.shape[1]
    width = whole // 2
    steps = arrived.shape[0] // rows
    tails = arrived[:, whole:]
    for which, out in ((0, retain), (1, slope)):
        terms = mm(tails, unpack(half[0], width, which)).reshape(steps, rows, width)
        out[...] = (terms[:, 0] + terms[:, 1]) + terms[:, 2]
    retain[...] = jnp.exp(retain[...])
    states[...] = arrived[:, :whole].astype(F32)
    state = jnp.zeros((rows, width), F32)
    state_dot = jnp.zeros((rows, width), F32)
    for j in range(steps):
        own = slice(j * rows, (j + 1) * rows)
        arriving, arriving_dot = states[own, :width], states[own, width:]
        states[own, :width] = state
        states[own, width:] = state_dot
        r = retain[j : j + 1, :]
        state_dot = r * (state_dot + slope[j : j + 1, :] * state) + arriving_dot
        state = r * state + arriving
    leaving[...] = states[...].astype(BF16)


def arrange_body(place, w_t, keep, send):
    rows = w_t.shape[0] // (2 * CHIPS)
    for d in range(CHIPS):
        own = slice(d * rows, (d + 1) * rows)
        for other, out in ((False, keep), (True, send)):
            at = pl.multiple_of(group(place, d, other) * rows, rows)
            out[own, :] = w_t[pl.ds(at, rows), :]


def own_body(keep, own, out):
    for b in range(own.shape[1] // SPAN):
        lanes = slice(b * SPAN, (b + 1) * SPAN)
        out[:, lanes] = mm(keep[...], own[:, lanes])


def product_body(begun, received, other, *outs):
    rows = outs[0].shape[0]
    for b in range(other.shape[1] // SPAN):
        lanes = slice(b * SPAN, (b + 1) * SPAN)
        result = begun[:, lanes] + mm(received[...], other[:, lanes])
        for d, out in enumerate(outs):
            out[:, lanes] = result[d * rows : (d + 1) * rows].astype(BF16)


def read_body(
    copies, arrived, first, second, first_dot, second_dot, within, within_dot, table, vec, s0, s0_dot,
    inner, inner_dot, readers, readers_dot, sems,
):
    n = readers.shape[0]
    reading = []
    for i, (source, out) in enumerate(
        ((first, readers), (second, readers), (first_dot, readers_dot), (second_dot, readers_dot))
    ):
        lanes = slice((i % 2) * SPAN, (i % 2 + 1) * SPAN)
        reading.append(
            pltpu.make_async_copy(
                source.at[source.shape[0] - n :, :], out.at[:, lanes], sems.at[i]
            )
        )
    for copy in reading:
        copy.start()
    for copy in [*copies, *reading]:
        copy.wait()
    width = within.shape[0]
    entry = from_owners(arrived[:, : width // 2].astype(F32))
    entry_dot = from_owners(arrived[:, width // 2 :].astype(F32))
    for b in range(2):
        lanes = slice(b * SPAN, (b + 1) * SPAN)
        reader, reader_dot = readers[:, lanes], readers_dot[:, lanes]
        rounded = jnp.concatenate([entry.astype(BF16), entry_dot.astype(BF16)], 0)
        read = mm(rounded[: entry.shape[0]], reader, TN)
        read_dot = mm(rounded, jnp.concatenate([reader_dot, reader], 0), TN)
        for h in range(width // HEAD_DIM):
            rows = slice(h * HEAD_DIM, (h + 1) * HEAD_DIM)
            e = table[CUM_EXP + h : CUM_EXP + h + 1, lanes]
            d = table[CUM_DOT + h : CUM_DOT + h + 1, lanes]
            inner[rows, lanes] = (within[rows, lanes] + e * read[rows]).astype(BF16)
            inner_dot[rows, lanes] = (
                within_dot[rows, lanes] + e * (read_dot[rows] + d * read[rows])
            ).astype(BF16)
        if b == 0:
            retain, slope = vec[0:1, :], vec[1:2, :]
            entry_dot = retain * (entry_dot + slope * entry) + s0_dot[...]
            entry = retain * entry + s0[...]


def total_body(*refs):
    out = refs[-1]
    summed = refs[0][...].astype(F32)
    for ref in refs[1:-1]:
        summed = summed + ref[...].astype(F32)
    out[...] = summed.astype(BF16)


def on_device(
    tokens,
    tangent_tokens,
    log_decay,
    tangent_decay,
    w_inner,
    w_bmat,
    w_cmat,
    conv_inner,
    conv_bc,
    skip_gain,
    w_out,
):
    length, piece = tokens.shape
    model, width = w_inner.shape
    state_len = w_bmat.shape[1]
    channels = width + 2 * state_len
    heads = width // HEAD_DIM
    n_ctx, n_head = lax.axis_size("ctx"), lax.axis_size("head")
    chips = n_head // 2
    margin = conv_inner.shape[0] - 1
    shape = jax.ShapeDtypeStruct
    place = lax.axis_index("head")

    def along(values, distance):
        route = [
            (2 * i + j, 2 * ((i + distance) % chips) + j) for i in range(chips) for j in range(2)
        ]
        return lax.ppermute(values, "head", route)

    def swap(values):
        return lax.ppermute(values, "head", [(i, i ^ 1) for i in range(n_head)])

    def exchange(values):
        blocks = values.reshape(n_ctx, values.shape[0] // n_ctx, values.shape[1])
        return lax.all_to_all(blocks, "ctx", 0, 0).reshape(values.shape)

    first, second = tokens.T, tangent_tokens.T
    first_up, first_down = along(first, 1), along(first, -1)

    second_down = along(second, -1)
    pad = ((0, 16 - heads), (0, 0))
    dec = jnp.concatenate([jnp.pad(log_decay.T, pad), jnp.pad(tangent_decay.T, pad)], 0)
    table, columns, vec, tail = call(
        decay_body,
        [shape((80, length), F32), shape((length, 32), F32)]
        + [shape((8, width), F32), shape((8, 128), F32)],
        pinned=True,
        count=1,
        work=(10**8, 10**6),
    )(dec)
    first_up, table = lax.optimization_barrier((first_up, table))
    first_far = along(first_up, 1)
    later, first_far = lax.optimization_barrier((second, first_far))
    second_up = along(later, 1)
    second_far = along(second_down, -1)
    firsts = [first, first_up, first_down, first_far]
    firsts = firsts + [swap(v) for v in firsts]
    here = place[None]
    taps = jnp.concatenate([conv_inner, conv_bc], 1)

    full = [pltpu.VMEM((model, length), BF16), pltpu.VMEM((model, channels), BF16)]
    full += [pltpu.VMEM((length, channels), F32)]
    work = (2 * channels * model * length, 12 * MIB)
    tokens_by = shape((length, channels), BF16)
    (projected,) = call(
        primal_body,
        [tokens_by],
        [*full, pltpu.SemaphoreType.DMA((14,))],
        held=tuple(range(1, 12)),
        loose=tuple(range(1, 9)),
        count=12,
        smem=(0,),
        work=work,
        limit=BIG,
    )(here, *firsts, w_inner, w_bmat, w_cmat)
    second_up, second_far, projected = lax.optimization_barrier(
        (second_up, second_far, projected)
    )
    seconds = [second, second_up, second_down, second_far]
    seconds = seconds + [swap(second), swap(second_up), swap(second_down), swap(second_far)]
    projected_dot, edge = call(
        tangent_body,
        [tokens_by, shape((16, channels), BF16)],
        [*full, pltpu.VMEM((16, channels), BF16), pltpu.SemaphoreType.DMA((15,))],
        near=(12,),
        held=tuple(range(1, 13)),
        loose=tuple(range(1, 9)),
        count=13,
        smem=(0,),
        work=work,
        limit=BIG,
    )(here, *seconds, w_inner, w_bmat, w_cmat, projected)
    before = lax.ppermute(edge, "ctx", [(i, i + 1) for i in range(n_ctx - 1)])
    mix = shape((channels, SPAN), BF16)
    state = shape((state_len, width), F32)

    def block(b, out, *more):
        args = (projected, projected_dot, taps, table, vec, tail, *more)
        return call(
            functools.partial(block_body, b),
            [mix, mix, state, state, *out],
            [pltpu.VMEM((SPAN + 8, channels), F32)] * 2
            + [pltpu.VMEM((SPAN, channels), F32)]
            + [pltpu.VMEM((SPAN, channels), BF16)] * 2
            + [pltpu.VMEM((width, 2 * SPAN), BF16)],
            near=(0, 1, 2, 7, 8),
            pinned=(0, 1, 2, 3, 4) if out else (0, 1),
            count=len(args),
            work=(10**9, 8 * MIB),
            limit=20,
        )(*args)

    mixed1, mixed1_dot, state1, state1_dot = block(1, [])
    mixed0, mixed0_dot, state0, state0_dot, message = block(
        0, [shape((2 * state_len, width + 128), BF16)], before, state1, state1_dot
    )

    arrived = exchange(message)
    gains = jnp.pad(skip_gain[None], ((0, 0), (0, 16 - heads)))
    wide = shape((width, length), F32)
    within, within_dot = call(
        within_body,
        [wide, wide],
        [pltpu.VMEM((SPAN, SPAN), F32)] * 2,
        pinned=True,
        count=7,
        work=(5 * 10**9, 8 * MIB),
        limit=BIG,
    )(mixed0, mixed1, mixed0_dot, mixed1_dot, table, columns, gains)
    half = (lax.axis_index("ctx") % 2).astype(jnp.int32)[None]
    line = pltpu.VMEM((n_ctx, width // 2), F32)
    (leaving,) = call(
        scan_body,
        [shape((2 * state_len, width), BF16)],
        [pltpu.VMEM((2 * state_len, width), F32), line, line],
        near=(1,),
        count=2,
        smem=(0,),
        work=(10**8, MIB),
    )(half, arrived)
    entry = exchange(leaving)

    side = shape((model // 2, width), BF16)
    keep, send = call(
        arrange_body, [side, side], near=(1,), count=2, smem=(0,), work=(10**6, 6 * MIB)
    )(here, w_out.T)
    received = swap(send)
    values = shape((width, length), BF16)
    reader = pltpu.VMEM((state_len, length), BF16)
    inner, inner_dot = call(
        read_body,
        [values, values],
        [reader, reader, pltpu.SemaphoreType.DMA((4,))],
        near=(0,),
        held=(1, 2, 3, 4),
        count=11,
        work=(10**9, 6 * MIB),
        limit=BIG,
    )(
        entry, mixed0, mixed1, mixed0_dot, mixed1_dot, within, within_dot, table, vec, state0,
        state0_dot,
    )
    term = shape((piece, length), BF16)
    work = (2 * chips * piece * width * length, 4 * MIB)
    begin = call(
        own_body, [shape((chips * piece, length), F32)], near=(0, 1), count=2, work=work
    )
    product = call(product_body, [term] * chips, near=(0, 1, 2), count=3, work=work)

    def total(*terms):
        count = len(terms)
        body = call(total_body, [term], near=range(count), count=count, work=(10**6, 2 * MIB))
        return body(*terms)[0]

    def finish(begun, other, way):
        terms = product(begun, received, other)
        far = along(terms[2], way)
        near, back = (terms[1], terms[3]) if way == 1 else (terms[3], terms[1])
        back = along(back, -way)
        near = along(total(near, far), way)
        return total(terms[0], near, back).T

    other, other_dot = swap(inner), swap(inner_dot)
    begun, begun_dot = begin(keep, inner)[0], begin(keep, inner_dot)[0]
    return finish(begun, other, 1), finish(begun_dot, other_dot, -1)


def solution(mesh):
    in_specs = (
        P("ctx", "head"),
        P("ctx", "head"),
        P("ctx", "head"),
        P("ctx", "head"),
        P(None, "head"),
        P(),
        P(),
        P(None, "head"),
        P(),
        P("head"),
        P("head", None),
    )
    out_specs = (P("ctx", "head"), P("ctx", "head"))
    return jax.shard_map(
        on_device, mesh=mesh, in_specs=in_specs, out_specs=out_specs, check_vma=False
    )
```

```python
import functools

import jax
import jax.numpy as jnp
from jax import lax
from jax.experimental import pallas as pl
from jax.experimental.pallas import tpu as pltpu
from jax.sharding import PartitionSpec as P

HEAD_DIM = 64
SPAN = 256
MIB = 1 << 20
BIG = 24
CHIPS = 4
AROUND = (0, CHIPS - 1, 1, 2)
BF16 = jnp.bfloat16
F32 = jnp.float32
HIGHEST = lax.Precision.HIGHEST

NN = (((1,), (0,)), ((), ()))
NT = (((1,), (1,)), ((), ()))
TN = (((0,), (0,)), ((), ()))


def mm(a, b, dims=NN, precision=None):
    return lax.dot_general(a, b, dims, precision=precision, preferred_element_type=F32)


def call(body, out, scratch=(), smem=(), near=(), held=(), loose=(), pinned=(), count=0, work=(0, 0), limit=16):
    outs = list(out)
    n_out, n_scratch = len(outs), len(scratch)
    far = [i for i in range(count) if i not in smem and i not in held and i not in near]
    far_out = list(range(n_out)) if pinned is True else list(pinned)

    def kernel(*refs):
        ins, res = list(refs[:count]), list(refs[count : count + n_out])
        rest = refs[count + n_out :]
        own, rest = list(rest[:n_scratch]), list(rest[n_scratch:])
        copies, late = [], []
        for k, i in enumerate(far):
            copies.append(pltpu.make_async_copy(ins[i], rest[k], rest[-1].at[k]))
            ins[i] = rest[k]
        for k, i in enumerate(far_out, len(far)):
            late.append(pltpu.make_async_copy(rest[k], res[i], rest[-1].at[k]))
            res[i] = rest[k]
        for copy in copies:
            copy.start()
        if held:
            body(copies, *ins, *res, *own)
        else:
            for copy in copies:
                copy.wait()
            body(*ins, *res, *own)
        for copy in late:
            copy.start()
        for copy in late:
            copy.wait()

    def space(i):
        if i in smem:
            return pltpu.SMEM
        return pltpu.VMEM if i in near else pl.ANY if i in loose else pltpu.HBM

    def run(*args):
        assert len(args) == count
        buffers = [pltpu.VMEM(args[i].shape, args[i].dtype) for i in far]
        args = [
            pltpu.with_memory_space_constraint(v, pltpu.HBM) if space(i) is pltpu.HBM else v
            for i, v in enumerate(args)
        ]
        buffers += [pltpu.VMEM(outs[i].shape, outs[i].dtype) for i in far_out]
        if buffers:
            buffers.append(pltpu.SemaphoreType.DMA((len(buffers),)))
        return pl.pallas_call(
            kernel,
            out_shape=[
                pltpu.HBM(v.shape, v.dtype) if i in far_out else v for i, v in enumerate(outs)
            ],
            in_specs=[pl.BlockSpec(memory_space=space(i)) for i in range(count)],
            out_specs=[
                pl.BlockSpec(memory_space=pltpu.HBM if i in far_out else pltpu.VMEM)
                for i in range(n_out)
            ],
            scratch_shapes=list(scratch) + buffers,
            cost_estimate=pl.CostEstimate(
                flops=work[0], bytes_accessed=work[1], transcendentals=0
            ),
            compiler_params=pltpu.CompilerParams(vmem_limit_bytes=limit * MIB),
        )(*args)

    return run


def spread(rows, width):
    head = lax.broadcasted_iota(jnp.int32, (rows, width), 0)
    lane = lax.broadcasted_iota(jnp.int32, (rows, width), 1)
    return jnp.where(lane // HEAD_DIM == head, 1.0, 0.0).astype(F32)


CUM, CUM_DOT, REM, REM_DOT, CUM_EXP = 0, 16, 32, 48, 64


def decay_body(dec, table, columns, vec, tail):
    s = lax.broadcasted_iota(jnp.int32, (SPAN, SPAN), 0)
    t = lax.broadcasted_iota(jnp.int32, (SPAN, SPAN), 1)
    upper = jnp.where(s <= t, 1.0, 0.0).astype(F32)
    lower = jnp.where(t <= s, 1.0, 0.0).astype(F32)
    ends = []
    for b in range(dec.shape[1] // SPAN):
        lanes = slice(b * SPAN, (b + 1) * SPAN)
        both = dec[:, lanes]
        c = mm(both, upper, NN, HIGHEST)
        c_t = mm(lower, both, NT, HIGHEST)
        p, d = c[:16], c[16:]
        table[CUM : CUM + 16, lanes] = p
        table[CUM_DOT : CUM_DOT + 16, lanes] = d
        table[CUM_EXP : CUM_EXP + 16, lanes] = jnp.exp(p)
        r = jnp.exp(p[:, SPAN - 1 :] - p)
        table[REM : REM + 16, lanes] = r
        table[REM_DOT : REM_DOT + 16, lanes] = r * (d[:, SPAN - 1 :] - d)
        columns[lanes, :] = c_t
        ends.append(c_t[SPAN - 1 :, :])
    rows = jnp.concatenate(
        [ends[0][:, :16], ends[0][:, 16:], ends[1][:, :16], ends[1][:, 16:]]
        + [jnp.zeros((4, 16), F32)],
        0,
    )
    wide = mm(rows, spread(16, vec.shape[1]), NN, HIGHEST)
    row = lax.broadcasted_iota(jnp.int32, wide.shape, 0)
    vec[...] = jnp.where((row == 0) | (row == 2), jnp.exp(wide), wide)
    rest = ends[0] + ends[1]
    tail[...] = jnp.zeros(tail.shape, F32)
    for i in range(3):
        term = rest.astype(BF16).astype(F32)
        tail[i : i + 1, 0:32] = term
        rest = rest - term


def group(place, distance, other):
    chip, core = place[0] // 2, place[0] % 2
    return (chip + distance) % CHIPS * 2 + (1 - core if other else core)


def gather(place, pieces, full, sems):
    rows = pieces[0].shape[0]
    arriving = []
    for i, piece in enumerate(pieces):
        at = group(place, AROUND[i % 4], i >= 4) * rows
        here = full.at[pl.ds(pl.multiple_of(at, rows), rows), :]
        arriving.append(pltpu.make_async_copy(piece, here, sems.at[i]))
    for copy in arriving:
        copy.start()
    return arriving


CHUNK = 64


def convolve(ext, taps, store):
    count = taps.shape[0]
    for c in range(taps.shape[1] // 128):
        lanes = slice(c * 128, (c + 1) * 128)
        kernel = [jnp.broadcast_to(taps[k : k + 1, lanes], (CHUNK, 128)) for k in range(count)]
        for r in range(0, SPAN, CHUNK):
            summed = None
            for k in range(count):
                at = r + 9 - count + k
                term = kernel[k] * ext[at : at + CHUNK, lanes]
                summed = term if summed is None else summed + term
            store(slice(r, r + CHUNK), lanes, summed)


def turn(rows):
    s = lax.broadcasted_iota(jnp.int32, (SPAN, SPAN), 0)
    t = lax.broadcasted_iota(jnp.int32, (SPAN, SPAN), 1)
    return mm(rows, jnp.where(s == t, 1.0, 0.0).astype(BF16), TN).astype(BF16)


def to_owners(values):
    n, width = values.shape
    halves = [values[:, : width // 2], values[:, width // 2 :]]
    stacked = jnp.stack([v.reshape(n // 8, 8, width // 2) for v in halves], 1)
    return stacked.reshape(2 * n, width // 2)


def from_owners(values):
    n, width = values.shape
    split = values.reshape(n // 16, 2, 8, width)
    return jnp.concatenate([split[:, i].reshape(n // 2, width) for i in range(2)], 1)


def project(place, pieces, weights, out, full, w_all, total, sems):
    arriving = gather(place, pieces, full, sems)
    half = w_all.shape[0] // 2
    coming = []
    for part in range(2):
        rows = slice(part * half, (part + 1) * half)
        at = 0
        for i, weight in enumerate(weights):
            columns = slice(at, at + weight.shape[1])
            at = columns.stop
            copy = pltpu.make_async_copy(
                weight.at[rows, :], w_all.at[rows, columns], sems.at[8 + 3 * part + i]
            )
            copy.start()
            coming.append(copy)
    for copy in [*arriving, *coming[:3]]:
        copy.wait()
    total[...] = mm(full[:half, :], w_all[:half, :], TN)
    for copy in coming[3:]:
        copy.wait()
    out[...] = (total[...] + mm(full[half:, :], w_all[half:, :], TN)).astype(BF16)


def primal_body(copies, place, *refs):
    project(place, refs[:8], refs[8:11], *refs[11:])


def tangent_body(copies, place, *refs):
    first, projected, edge, full, w_all, total, last, sems = refs[11:]
    length = full.shape[1]
    ending = pltpu.make_async_copy(first.at[length - 16 :, :], last, sems.at[14])
    ending.start()
    project(place, refs[:8], refs[8:11], projected, full, w_all, total, sems)
    ending.wait()
    ends = [last[...].astype(F32)[8:], projected[length - 16 :, :].astype(F32)[8:]]
    edge[...] = jnp.concatenate(ends, 0).astype(BF16)


def block_body(b, projected, projected_dot, taps, table, vec, tail, *refs):
    if b == 0:
        before, state1, state1_dot, mixed, mixed_dot, state, state_dot, message = refs[:8]
        refs = refs[8:]
    else:
        mixed, mixed_dot, state, state_dot = refs[:4]
        refs = refs[4:]
    ext, ext_dot, gate, rows, rows_dot, scaled = refs
    at = slice(b * SPAN, (b + 1) * SPAN)
    for i, (source, out) in enumerate(((projected, ext), (projected_dot, ext_dot))):
        if b > 0:
            ahead = source[b * SPAN - 16 : b * SPAN, :].astype(F32)[8:]
        else:
            ahead = before[...].astype(F32)[8 * i : 8 * i + 8]
        out[0:8, :] = ahead
        out[8:, :] = source[at, :].astype(F32)

    def store(where, lanes, v):
        sig = 0.5 + 0.5 * jnp.tanh(0.5 * v)
        rows[where, lanes] = (v * sig).astype(BF16)
        gate[where, lanes] = sig * (1.0 + v * (1.0 - sig))

    def store_dot(where, lanes, v):
        rows_dot[where, lanes] = (gate[where, lanes] * v).astype(BF16)

    convolve(ext, taps, store)
    mixed[...] = turn(rows[...])
    convolve(ext_dot, taps, store_dot)
    mixed_dot[...] = turn(rows_dot[...])
    width = vec.shape[1]
    for h in range(width // HEAD_DIM):
        here = slice(h * HEAD_DIM, (h + 1) * HEAD_DIM)
        value = mixed[here, :].astype(F32)
        r = table[REM + h : REM + h + 1, at]
        scaled[here, SPAN:] = (value * r).astype(BF16)
        scaled[here, :SPAN] = (
            mixed_dot[here, :].astype(F32) * r + value * table[REM_DOT + h : REM_DOT + h + 1, at]
        ).astype(BF16)
    writer = mixed[width : width + 128, :]
    writer_dot = mixed_dot[width : width + 128, :]
    own = mm(writer, scaled[:, SPAN:], NT)
    own_dot = mm(jnp.concatenate([writer, writer_dot], 1), scaled[...], NT)
    state[...] = own
    state_dot[...] = own_dot
    if b == 0:
        own_dot = vec[2:3, :] * (own_dot + vec[3:4, :] * own) + state1_dot[...]
        own = vec[2:3, :] * own + state1[...]
        message[:, : width // 2] = to_owners(own).astype(BF16)
        message[:, width // 2 : width] = to_owners(own_dot).astype(BF16)
        both = jnp.concatenate([tail[...], tail[...]], 0).astype(BF16)
        for j in range(message.shape[0] // 16):
            message[16 * j : 16 * j + 16, width:] = both


def within_body(first, second, first_dot, second_dot, table, columns, gain, within, within_dot, sc, scd):
    width = within.shape[0]
    state = (first.shape[0] - width) // 2
    s = lax.broadcasted_iota(jnp.int32, (SPAN, SPAN), 0)
    t = lax.broadcasted_iota(jnp.int32, (SPAN, SPAN), 1)
    causal = s <= t
    for b in range(2):
        lanes = slice(b * SPAN, (b + 1) * SPAN)
        mixed, mixed_dot = ((first, first_dot), (second, second_dot))[b]
        writer, reader = mixed[width : width + state, :], mixed[width + state :, :]
        writer_dot, reader_dot = mixed_dot[width : width + state, :], mixed_dot[width + state :, :]
        sc[...] = mm(writer, reader, TN)
        scd[...] = mm(jnp.concatenate([writer_dot, writer], 0), jnp.concatenate([reader, reader_dot], 0), TN)
        for h in range(width // HEAD_DIM):
            rows = slice(h * HEAD_DIM, (h + 1) * HEAD_DIM)
            diff = table[CUM + h : CUM + h + 1, lanes] - columns[lanes, h : h + 1]
            diff_dot = (
                table[CUM_DOT + h : CUM_DOT + h + 1, lanes] - columns[lanes, 16 + h : 17 + h]
            )
            weight = jnp.exp(jnp.where(causal, diff, -jnp.inf))
            mix = (weight * sc[...]).astype(BF16)
            mix_dot = (weight * (scd[...] + diff_dot * sc[...])).astype(BF16)
            value, value_dot = mixed[rows, :], mixed_dot[rows, :]
            both = mm(jnp.concatenate([value, value_dot], 0), mix)
            other = mm(value, mix_dot)
            skip = gain[0:1, h : h + 1]
            within[rows, lanes] = both[:HEAD_DIM] + skip * value.astype(F32)
            within_dot[rows, lanes] = (both[HEAD_DIM:] + other) + skip * value_dot.astype(F32)


def unpack(half, width, which):
    lane = lax.broadcasted_iota(jnp.int32, (128, width), 0)
    head = lax.broadcasted_iota(jnp.int32, (128, width), 1) // HEAD_DIM + half * (width // HEAD_DIM)
    return jnp.where(lane == head + 16 * which, 1.0, 0.0).astype(BF16)


def scan_body(half, arrived, leaving, states, retain, slope):
    rows, whole = 8, leaving.shape[1]
    width = whole // 2
    steps = arrived.shape[0] // rows
    tails = arrived[:, whole:]
    for which, out in ((0, retain), (1, slope)):
        terms = mm(tails, unpack(half[0], width, which)).reshape(steps, rows, width)
        out[...] = (terms[:, 0] + terms[:, 1]) + terms[:, 2]
    retain[...] = jnp.exp(retain[...])
    states[...] = arrived[:, :whole].astype(F32)
    state = jnp.zeros((rows, width), F32)
    state_dot = jnp.zeros((rows, width), F32)
    for j in range(steps):
        own = slice(j * rows, (j + 1) * rows)
        arriving, arriving_dot = states[own, :width], states[own, width:]
        states[own, :width] = state
        states[own, width:] = state_dot
        r = retain[j : j + 1, :]
        state_dot = r * (state_dot + slope[j : j + 1, :] * state) + arriving_dot
        state = r * state + arriving
    leaving[...] = states[...].astype(BF16)


def arrange_body(place, w_t, keep, send):
    rows = w_t.shape[0] // (2 * CHIPS)
    for d in range(CHIPS):
        own = slice(d * rows, (d + 1) * rows)
        for other, out in ((False, keep), (True, send)):
            at = pl.multiple_of(group(place, d, other) * rows, rows)
            out[own, :] = w_t[pl.ds(at, rows), :]


def own_body(keep, own, out):
    for b in range(own.shape[1] // SPAN):
        lanes = slice(b * SPAN, (b + 1) * SPAN)
        out[:, lanes] = mm(keep[...], own[:, lanes])


def product_body(begun, received, other, *outs):
    rows = outs[0].shape[0]
    for b in range(other.shape[1] // SPAN):
        lanes = slice(b * SPAN, (b + 1) * SPAN)
        result = begun[:, lanes] + mm(received[...], other[:, lanes])
        for d, out in enumerate(outs):
            out[:, lanes] = result[d * rows : (d + 1) * rows].astype(BF16)


def read_body(
    copies, arrived, first, second, first_dot, second_dot, within, within_dot, table, vec, s0, s0_dot,
    inner, inner_dot, readers, readers_dot, sems,
):
    n = readers.shape[0]
    reading = []
    for i, (source, out) in enumerate(
        ((first, readers), (second, readers), (first_dot, readers_dot), (second_dot, readers_dot))
    ):
        lanes = slice((i % 2) * SPAN, (i % 2 + 1) * SPAN)
        reading.append(
            pltpu.make_async_copy(
                source.at[source.shape[0] - n :, :], out.at[:, lanes], sems.at[i]
            )
        )
    for copy in reading:
        copy.start()
    for copy in [*copies, *reading]:
        copy.wait()
    width = within.shape[0]
    entry = from_owners(arrived[:, : width // 2].astype(F32))
    entry_dot = from_owners(arrived[:, width // 2 :].astype(F32))
    for b in range(2):
        lanes = slice(b * SPAN, (b + 1) * SPAN)
        reader, reader_dot = readers[:, lanes], readers_dot[:, lanes]
        rounded = jnp.concatenate([entry.astype(BF16), entry_dot.astype(BF16)], 0)
        read = mm(rounded[: entry.shape[0]], reader, TN)
        read_dot = mm(rounded, jnp.concatenate([reader_dot, reader], 0), TN)
        for h in range(width // HEAD_DIM):
            rows = slice(h * HEAD_DIM, (h + 1) * HEAD_DIM)
            e = table[CUM_EXP + h : CUM_EXP + h + 1, lanes]
            d = table[CUM_DOT + h : CUM_DOT + h + 1, lanes]
            inner[rows, lanes] = (within[rows, lanes] + e * read[rows]).astype(BF16)
            inner_dot[rows, lanes] = (
                within_dot[rows, lanes] + e * (read_dot[rows] + d * read[rows])
            ).astype(BF16)
        if b == 0:
            retain, slope = vec[0:1, :], vec[1:2, :]
            entry_dot = retain * (entry_dot + slope * entry) + s0_dot[...]
            entry = retain * entry + s0[...]


def total_body(*refs):
    out = refs[-1]
    summed = refs[0][...].astype(F32)
    for ref in refs[1:-1]:
        summed = summed + ref[...].astype(F32)
    out[...] = summed.astype(BF16)


def on_device(
    tokens,
    tangent_tokens,
    log_decay,
    tangent_decay,
    w_inner,
    w_bmat,
    w_cmat,
    conv_inner,
    conv_bc,
    skip_gain,
    w_out,
):
    length, piece = tokens.shape
    model, width = w_inner.shape
    state_len = w_bmat.shape[1]
    channels = width + 2 * state_len
    heads = width // HEAD_DIM
    n_ctx, n_head = lax.axis_size("ctx"), lax.axis_size("head")
    chips = n_head // 2
    margin = conv_inner.shape[0] - 1
    shape = jax.ShapeDtypeStruct
    place = lax.axis_index("head")

    def along(values, distance):
        route = [
            (2 * i + j, 2 * ((i + distance) % chips) + j) for i in range(chips) for j in range(2)
        ]
        return lax.ppermute(values, "head", route)

    def swap(values):
        return lax.ppermute(values, "head", [(i, i ^ 1) for i in range(n_head)])

    def exchange(values):
        blocks = values.reshape(n_ctx, values.shape[0] // n_ctx, values.shape[1])
        return lax.all_to_all(blocks, "ctx", 0, 0).reshape(values.shape)

    first, second = tokens.T, tangent_tokens.T
    first_up, first_down = along(first, 1), along(first, -1)

    second_down = along(second, -1)
    pad = ((0, 16 - heads), (0, 0))
    dec = jnp.concatenate([jnp.pad(log_decay.T, pad), jnp.pad(tangent_decay.T, pad)], 0)
    table, columns, vec, tail = call(
        decay_body,
        [shape((80, length), F32), shape((length, 32), F32)]
        + [shape((8, width), F32), shape((8, 128), F32)],
        pinned=True,
        count=1,
        work=(10**8, 10**6),
    )(dec)
    first_up, table = lax.optimization_barrier((first_up, table))
    first_far = along(first_up, 1)
    later, first_far = lax.optimization_barrier((second, first_far))
    second_up = along(later, 1)
    second_far = along(second_down, -1)
    firsts = [first, first_up, first_down, first_far]
    firsts = firsts + [swap(v) for v in firsts]
    here = place[None]
    taps = jnp.concatenate([conv_inner, conv_bc], 1)

    full = [pltpu.VMEM((model, length), BF16), pltpu.VMEM((model, channels), BF16)]
    full += [pltpu.VMEM((length, channels), F32)]
    work = (2 * channels * model * length, 12 * MIB)
    tokens_by = shape((length, channels), BF16)
    (projected,) = call(
        primal_body,
        [tokens_by],
        [*full, pltpu.SemaphoreType.DMA((14,))],
        held=tuple(range(1, 12)),
        loose=tuple(range(2, 9)),
        count=12,
        smem=(0,),
        work=work,
        limit=BIG,
    )(here, *firsts, w_inner, w_bmat, w_cmat)
    second_up, second_far, projected = lax.optimization_barrier(
        (second_up, second_far, projected)
    )
    seconds = [second, second_up, second_down, second_far]
    seconds = seconds + [swap(second), swap(second_up), swap(second_down), swap(second_far)]
    projected_dot, edge = call(
        tangent_body,
        [tokens_by, shape((16, channels), BF16)],
        [*full, pltpu.VMEM((16, channels), BF16), pltpu.SemaphoreType.DMA((15,))],
        near=(12,),
        held=tuple(range(1, 13)),
        loose=tuple(range(2, 9)),
        count=13,
        smem=(0,),
        work=work,
        limit=BIG,
    )(here, *seconds, w_inner, w_bmat, w_cmat, projected)
    before = lax.ppermute(edge, "ctx", [(i, i + 1) for i in range(n_ctx - 1)])
    mix = shape((channels, SPAN), BF16)
    state = shape((state_len, width), F32)

    def block(b, out, *more):
        args = (projected, projected_dot, taps, table, vec, tail, *more)
        return call(
            functools.partial(block_body, b),
            [mix, mix, state, state, *out],
            [pltpu.VMEM((SPAN + 8, channels), F32)] * 2
            + [pltpu.VMEM((SPAN, channels), F32)]
            + [pltpu.VMEM((SPAN, channels), BF16)] * 2
            + [pltpu.VMEM((width, 2 * SPAN), BF16)],
            near=(0, 1, 2, 6, 7, 8),
            pinned=(0, 1, 2, 3, 4) if out else (0, 1),
            count=len(args),
            work=(10**9, 8 * MIB),
            limit=20,
        )(*args)

    mixed1, mixed1_dot, state1, state1_dot = block(1, [])
    mixed0, mixed0_dot, state0, state0_dot, message = block(
        0, [shape((2 * state_len, width + 128), BF16)], before, state1, state1_dot
    )

    arrived = exchange(message)
    gains = jnp.pad(skip_gain[None], ((0, 0), (0, 16 - heads)))
    wide = shape((width, length), F32)
    within, within_dot = call(
        within_body,
        [wide, wide],
        [pltpu.VMEM((SPAN, SPAN), F32)] * 2,
        pinned=True,
        count=7,
        work=(5 * 10**9, 8 * MIB),
        limit=BIG,
    )(mixed0, mixed1, mixed0_dot, mixed1_dot, table, columns, gains)
    half = (lax.axis_index("ctx") % 2).astype(jnp.int32)[None]
    line = pltpu.VMEM((n_ctx, width // 2), F32)
    (leaving,) = call(
        scan_body,
        [shape((2 * state_len, width), BF16)],
        [pltpu.VMEM((2 * state_len, width), F32), line, line],
        near=(1,),
        count=2,
        smem=(0,),
        work=(10**8, MIB),
    )(half, arrived)
    entry = exchange(leaving)

    side = shape((model // 2, width), BF16)
    keep, send = call(
        arrange_body, [side, side], near=(1,), count=2, smem=(0,), work=(10**6, 6 * MIB)
    )(here, w_out.T)
    received = swap(send)
    values = shape((width, length), BF16)
    reader = pltpu.VMEM((state_len, length), BF16)
    inner, inner_dot = call(
        read_body,
        [values, values],
        [reader, reader, pltpu.SemaphoreType.DMA((4,))],
        near=(0,),
        held=(1, 2, 3, 4),
        count=11,
        work=(10**9, 6 * MIB),
        limit=BIG,
    )(
        entry, mixed0, mixed1, mixed0_dot, mixed1_dot, within, within_dot, table, vec, state0,
        state0_dot,
    )
    term = shape((piece, length), BF16)
    work = (2 * chips * piece * width * length, 4 * MIB)
    begin = call(
        own_body, [shape((chips * piece, length), F32)], near=(0, 1), count=2, work=work
    )
    product = call(product_body, [term] * chips, near=(0, 1, 2), count=3, work=work)

    def total(*terms):
        count = len(terms)
        body = call(total_body, [term], near=range(count), count=count, work=(10**6, 2 * MIB))
        return body(*terms)[0]

    def finish(begun, other, way):
        terms = product(begun, received, other)
        far = along(terms[2], way)
        near, back = (terms[1], terms[3]) if way == 1 else (terms[3], terms[1])
        back = along(back, -way)
        near = along(total(near, far), way)
        return total(terms[0], near, back).T

    other, other_dot = swap(inner), swap(inner_dot)
    begun, begun_dot = begin(keep, inner)[0], begin(keep, inner_dot)[0]
    return finish(begun, other, 1), finish(begun_dot, other_dot, -1)


def solution(mesh):
    in_specs = (
        P("ctx", "head"),
        P("ctx", "head"),
        P("ctx", "head"),
        P("ctx", "head"),
        P(None, "head"),
        P(),
        P(),
        P(None, "head"),
        P(),
        P("head"),
        P("head", None),
    )
    out_specs = (P("ctx", "head"), P("ctx", "head"))
    return jax.shard_map(
        on_device, mesh=mesh, in_specs=in_specs, out_specs=out_specs, check_vma=False
    )
```

```python
import functools

import jax
import jax.numpy as jnp
from jax import lax
from jax.experimental import pallas as pl
from jax.experimental.pallas import tpu as pltpu
from jax.sharding import PartitionSpec as P

HEAD_DIM = 64
SPAN = 256
MIB = 1 << 20
BIG = 24
CHIPS = 4
AROUND = (0, CHIPS - 1, 1, 2)
BF16 = jnp.bfloat16
F32 = jnp.float32
HIGHEST = lax.Precision.HIGHEST

NN = (((1,), (0,)), ((), ()))
NT = (((1,), (1,)), ((), ()))
TN = (((0,), (0,)), ((), ()))


def mm(a, b, dims=NN, precision=None):
    return lax.dot_general(a, b, dims, precision=precision, preferred_element_type=F32)


def call(body, out, scratch=(), smem=(), near=(), held=(), loose=(), pinned=(), count=0, work=(0, 0), limit=16):
    outs = list(out)
    n_out, n_scratch = len(outs), len(scratch)
    far = [i for i in range(count) if i not in smem and i not in held and i not in near]
    far_out = list(range(n_out)) if pinned is True else list(pinned)

    def kernel(*refs):
        ins, res = list(refs[:count]), list(refs[count : count + n_out])
        rest = refs[count + n_out :]
        own, rest = list(rest[:n_scratch]), list(rest[n_scratch:])
        copies, late = [], []
        for k, i in enumerate(far):
            copies.append(pltpu.make_async_copy(ins[i], rest[k], rest[-1].at[k]))
            ins[i] = rest[k]
        for k, i in enumerate(far_out, len(far)):
            late.append(pltpu.make_async_copy(rest[k], res[i], rest[-1].at[k]))
            res[i] = rest[k]
        for copy in copies:
            copy.start()
        if held:
            body(copies, *ins, *res, *own)
        else:
            for copy in copies:
                copy.wait()
            body(*ins, *res, *own)
        for copy in late:
            copy.start()
        for copy in late:
            copy.wait()

    def space(i):
        if i in smem:
            return pltpu.SMEM
        return pltpu.VMEM if i in near else pl.ANY if i in loose else pltpu.HBM

    def run(*args):
        assert len(args) == count
        buffers = [pltpu.VMEM(args[i].shape, args[i].dtype) for i in far]
        args = [
            pltpu.with_memory_space_constraint(v, pltpu.HBM) if space(i) is pltpu.HBM else v
            for i, v in enumerate(args)
        ]
        buffers += [pltpu.VMEM(outs[i].shape, outs[i].dtype) for i in far_out]
        if buffers:
            buffers.append(pltpu.SemaphoreType.DMA((len(buffers),)))
        return pl.pallas_call(
            kernel,
            out_shape=[
                pltpu.HBM(v.shape, v.dtype) if i in far_out else v for i, v in enumerate(outs)
            ],
            in_specs=[pl.BlockSpec(memory_space=space(i)) for i in range(count)],
            out_specs=[
                pl.BlockSpec(memory_space=pltpu.HBM if i in far_out else pltpu.VMEM)
                for i in range(n_out)
            ],
            scratch_shapes=list(scratch) + buffers,
            cost_estimate=pl.CostEstimate(
                flops=work[0], bytes_accessed=work[1], transcendentals=0
            ),
            compiler_params=pltpu.CompilerParams(vmem_limit_bytes=limit * MIB),
        )(*args)

    return run


def spread(rows, width):
    head = lax.broadcasted_iota(jnp.int32, (rows, width), 0)
    lane = lax.broadcasted_iota(jnp.int32, (rows, width), 1)
    return jnp.where(lane // HEAD_DIM == head, 1.0, 0.0).astype(F32)


CUM, CUM_DOT, REM, REM_DOT, CUM_EXP = 0, 16, 32, 48, 64


def decay_body(dec, table, columns, vec, tail):
    s = lax.broadcasted_iota(jnp.int32, (SPAN, SPAN), 0)
    t = lax.broadcasted_iota(jnp.int32, (SPAN, SPAN), 1)
    upper = jnp.where(s <= t, 1.0, 0.0).astype(F32)
    lower = jnp.where(t <= s, 1.0, 0.0).astype(F32)
    ends = []
    for b in range(dec.shape[1] // SPAN):
        lanes = slice(b * SPAN, (b + 1) * SPAN)
        both = dec[:, lanes]
        c = mm(both, upper, NN, HIGHEST)
        c_t = mm(lower, both, NT, HIGHEST)
        p, d = c[:16], c[16:]
        table[CUM : CUM + 16, lanes] = p
        table[CUM_DOT : CUM_DOT + 16, lanes] = d
        table[CUM_EXP : CUM_EXP + 16, lanes] = jnp.exp(p)
        r = jnp.exp(p[:, SPAN - 1 :] - p)
        table[REM : REM + 16, lanes] = r
        table[REM_DOT : REM_DOT + 16, lanes] = r * (d[:, SPAN - 1 :] - d)
        columns[lanes, :] = c_t
        ends.append(c_t[SPAN - 1 :, :])
    rows = jnp.concatenate(
        [ends[0][:, :16], ends[0][:, 16:], ends[1][:, :16], ends[1][:, 16:]]
        + [jnp.zeros((4, 16), F32)],
        0,
    )
    wide = mm(rows, spread(16, vec.shape[1]), NN, HIGHEST)
    row = lax.broadcasted_iota(jnp.int32, wide.shape, 0)
    vec[...] = jnp.where((row == 0) | (row == 2), jnp.exp(wide), wide)
    rest = ends[0] + ends[1]
    tail[...] = jnp.zeros(tail.shape, F32)
    for i in range(3):
        term = rest.astype(BF16).astype(F32)
        tail[i : i + 1, 0:32] = term
        rest = rest - term


def group(place, distance, other):
    chip, core = place[0] // 2, place[0] % 2
    return (chip + distance) % CHIPS * 2 + (1 - core if other else core)


def gather(place, pieces, full, sems):
    rows = pieces[0].shape[0]
    arriving = []
    for i, piece in enumerate(pieces):
        at = group(place, AROUND[i % 4], i >= 4) * rows
        here = full.at[pl.ds(pl.multiple_of(at, rows), rows), :]
        arriving.append(pltpu.make_async_copy(piece, here, sems.at[i]))
    for copy in arriving:
        copy.start()
    return arriving


CHUNK = 64


def convolve(ext, taps, store):
    count = taps.shape[0]
    for c in range(taps.shape[1] // 128):
        lanes = slice(c * 128, (c + 1) * 128)
        kernel = [jnp.broadcast_to(taps[k : k + 1, lanes], (CHUNK, 128)) for k in range(count)]
        for r in range(0, SPAN, CHUNK):
            summed = None
            for k in range(count):
                at = r + 9 - count + k
                term = kernel[k] * ext[at : at + CHUNK, lanes]
                summed = term if summed is None else summed + term
            store(slice(r, r + CHUNK), lanes, summed)


def turn(rows):
    s = lax.broadcasted_iota(jnp.int32, (SPAN, SPAN), 0)
    t = lax.broadcasted_iota(jnp.int32, (SPAN, SPAN), 1)
    return mm(rows, jnp.where(s == t, 1.0, 0.0).astype(BF16), TN).astype(BF16)


def to_owners(values):
    n, width = values.shape
    halves = [values[:, : width // 2], values[:, width // 2 :]]
    stacked = jnp.stack([v.reshape(n // 8, 8, width // 2) for v in halves], 1)
    return stacked.reshape(2 * n, width // 2)


def from_owners(values):
    n, width = values.shape
    split = values.reshape(n // 16, 2, 8, width)
    return jnp.concatenate([split[:, i].reshape(n // 2, width) for i in range(2)], 1)


def project(place, pieces, weights, out, full, w_all, total, sems):
    arriving = gather(place, pieces, full, sems)
    half = w_all.shape[0] // 2
    coming = []
    for part in range(2):
        rows = slice(part * half, (part + 1) * half)
        at = 0
        for i, weight in enumerate(weights):
            columns = slice(at, at + weight.shape[1])
            at = columns.stop
            copy = pltpu.make_async_copy(
                weight.at[rows, :], w_all.at[rows, columns], sems.at[8 + 3 * part + i]
            )
            copy.start()
            coming.append(copy)
    for copy in [*arriving, *coming[:3]]:
        copy.wait()
    total[...] = mm(full[:half, :], w_all[:half, :], TN)
    for copy in coming[3:]:
        copy.wait()
    out[...] = (total[...] + mm(full[half:, :], w_all[half:, :], TN)).astype(BF16)


def primal_body(copies, place, *refs):
    project(place, refs[:8], refs[8:11], *refs[11:])


def tangent_body(copies, place, *refs):
    first, projected, edge, full, w_all, total, last, sems = refs[11:]
    length = full.shape[1]
    ending = pltpu.make_async_copy(first.at[length - 16 :, :], last, sems.at[14])
    ending.start()
    project(place, refs[:8], refs[8:11], projected, full, w_all, total, sems)
    ending.wait()
    ends = [last[...].astype(F32)[8:], projected[length - 16 :, :].astype(F32)[8:]]
    edge[...] = jnp.concatenate(ends, 0).astype(BF16)


def block_body(b, projected, projected_dot, taps, table, vec, tail, *refs):
    if b == 0:
        before, state1, state1_dot, mixed, mixed_dot, state, state_dot, message = refs[:8]
        refs = refs[8:]
    else:
        mixed, mixed_dot, state, state_dot = refs[:4]
        refs = refs[4:]
    ext, ext_dot, gate, rows, rows_dot, scaled = refs
    at = slice(b * SPAN, (b + 1) * SPAN)
    for i, (source, out) in enumerate(((projected, ext), (projected_dot, ext_dot))):
        if b > 0:
            ahead = source[b * SPAN - 16 : b * SPAN, :].astype(F32)[8:]
        else:
            ahead = before[...].astype(F32)[8 * i : 8 * i + 8]
        out[0:8, :] = ahead
        out[8:, :] = source[at, :].astype(F32)

    def store(where, lanes, v):
        sig = 0.5 + 0.5 * jnp.tanh(0.5 * v)
        rows[where, lanes] = (v * sig).astype(BF16)
        gate[where, lanes] = sig * (1.0 + v * (1.0 - sig))

    def store_dot(where, lanes, v):
        rows_dot[where, lanes] = (gate[where, lanes] * v).astype(BF16)

    convolve(ext, taps, store)
    mixed[...] = turn(rows[...])
    convolve(ext_dot, taps, store_dot)
    mixed_dot[...] = turn(rows_dot[...])
    width = vec.shape[1]
    for h in range(width // HEAD_DIM):
        here = slice(h * HEAD_DIM, (h + 1) * HEAD_DIM)
        value = mixed[here, :].astype(F32)
        r = table[REM + h : REM + h + 1, at]
        scaled[here, SPAN:] = (value * r).astype(BF16)
        scaled[here, :SPAN] = (
            mixed_dot[here, :].astype(F32) * r + value * table[REM_DOT + h : REM_DOT + h + 1, at]
        ).astype(BF16)
    writer = mixed[width : width + 128, :]
    writer_dot = mixed_dot[width : width + 128, :]
    own = mm(writer, scaled[:, SPAN:], NT)
    own_dot = mm(jnp.concatenate([writer, writer_dot], 1), scaled[...], NT)
    state[...] = own
    state_dot[...] = own_dot
    if b == 0:
        own_dot = vec[2:3, :] * (own_dot + vec[3:4, :] * own) + state1_dot[...]
        own = vec[2:3, :] * own + state1[...]
        message[:, : width // 2] = to_owners(own).astype(BF16)
        message[:, width // 2 : width] = to_owners(own_dot).astype(BF16)
        both = jnp.concatenate([tail[...], tail[...]], 0).astype(BF16)
        for j in range(message.shape[0] // 16):
            message[16 * j : 16 * j + 16, width:] = both


def within_body(first, second, first_dot, second_dot, table, columns, gain, within, within_dot, sc, scd):
    width = within.shape[0]
    state = (first.shape[0] - width) // 2
    s = lax.broadcasted_iota(jnp.int32, (SPAN, SPAN), 0)
    t = lax.broadcasted_iota(jnp.int32, (SPAN, SPAN), 1)
    causal = s <= t
    for b in range(2):
        lanes = slice(b * SPAN, (b + 1) * SPAN)
        mixed, mixed_dot = ((first, first_dot), (second, second_dot))[b]
        writer, reader = mixed[width : width + state, :], mixed[width + state :, :]
        writer_dot, reader_dot = mixed_dot[width : width + state, :], mixed_dot[width + state :, :]
        sc[...] = mm(writer, reader, TN)
        scd[...] = mm(jnp.concatenate([writer_dot, writer], 0), jnp.concatenate([reader, reader_dot], 0), TN)
        for h in range(width // HEAD_DIM):
            rows = slice(h * HEAD_DIM, (h + 1) * HEAD_DIM)
            diff = table[CUM + h : CUM + h + 1, lanes] - columns[lanes, h : h + 1]
            diff_dot = (
                table[CUM_DOT + h : CUM_DOT + h + 1, lanes] - columns[lanes, 16 + h : 17 + h]
            )
            weight = jnp.exp(jnp.where(causal, diff, -jnp.inf))
            mix = (weight * sc[...]).astype(BF16)
            mix_dot = (weight * (scd[...] + diff_dot * sc[...])).astype(BF16)
            value, value_dot = mixed[rows, :], mixed_dot[rows, :]
            both = mm(jnp.concatenate([value, value_dot], 0), mix)
            other = mm(value, mix_dot)
            skip = gain[0:1, h : h + 1]
            within[rows, lanes] = both[:HEAD_DIM] + skip * value.astype(F32)
            within_dot[rows, lanes] = (both[HEAD_DIM:] + other) + skip * value_dot.astype(F32)


def unpack(half, width, which):
    lane = lax.broadcasted_iota(jnp.int32, (128, width), 0)
    head = lax.broadcasted_iota(jnp.int32, (128, width), 1) // HEAD_DIM + half * (width // HEAD_DIM)
    return jnp.where(lane == head + 16 * which, 1.0, 0.0).astype(BF16)


def scan_body(half, arrived, leaving, states, retain, slope):
    rows, whole = 8, leaving.shape[1]
    width = whole // 2
    steps = arrived.shape[0] // rows
    tails = arrived[:, whole:]
    for which, out in ((0, retain), (1, slope)):
        terms = mm(tails, unpack(half[0], width, which)).reshape(steps, rows, width)
        out[...] = (terms[:, 0] + terms[:, 1]) + terms[:, 2]
    retain[...] = jnp.exp(retain[...])
    states[...] = arrived[:, :whole].astype(F32)
    state = jnp.zeros((rows, width), F32)
    state_dot = jnp.zeros((rows, width), F32)
    for j in range(steps):
        own = slice(j * rows, (j + 1) * rows)
        arriving, arriving_dot = states[own, :width], states[own, width:]
        states[own, :width] = state
        states[own, width:] = state_dot
        r = retain[j : j + 1, :]
        state_dot = r * (state_dot + slope[j : j + 1, :] * state) + arriving_dot
        state = r * state + arriving
    leaving[...] = states[...].astype(BF16)


def arrange_body(place, w_t, keep, send):
    rows = w_t.shape[0] // (2 * CHIPS)
    for d in range(CHIPS):
        own = slice(d * rows, (d + 1) * rows)
        for other, out in ((False, keep), (True, send)):
            at = pl.multiple_of(group(place, d, other) * rows, rows)
            out[own, :] = w_t[pl.ds(at, rows), :]


def own_body(keep, own, out):
    for b in range(own.shape[1] // SPAN):
        lanes = slice(b * SPAN, (b + 1) * SPAN)
        out[:, lanes] = mm(keep[...], own[:, lanes])


def product_body(begun, received, other, *outs):
    rows = outs[0].shape[0]
    for b in range(other.shape[1] // SPAN):
        lanes = slice(b * SPAN, (b + 1) * SPAN)
        result = begun[:, lanes] + mm(received[...], other[:, lanes])
        for d, out in enumerate(outs):
            out[:, lanes] = result[d * rows : (d + 1) * rows].astype(BF16)


def read_body(
    copies, arrived, first, second, first_dot, second_dot, within, within_dot, table, vec, s0, s0_dot,
    inner, inner_dot, readers, readers_dot, sems,
):
    n = readers.shape[0]
    reading = []
    for i, (source, out) in enumerate(
        ((first, readers), (second, readers), (first_dot, readers_dot), (second_dot, readers_dot))
    ):
        lanes = slice((i % 2) * SPAN, (i % 2 + 1) * SPAN)
        reading.append(
            pltpu.make_async_copy(
                source.at[source.shape[0] - n :, :], out.at[:, lanes], sems.at[i]
            )
        )
    for copy in reading:
        copy.start()
    for copy in [*copies, *reading]:
        copy.wait()
    width = within.shape[0]
    entry = from_owners(arrived[:, : width // 2].astype(F32))
    entry_dot = from_owners(arrived[:, width // 2 :].astype(F32))
    for b in range(2):
        lanes = slice(b * SPAN, (b + 1) * SPAN)
        reader, reader_dot = readers[:, lanes], readers_dot[:, lanes]
        rounded = jnp.concatenate([entry.astype(BF16), entry_dot.astype(BF16)], 0)
        read = mm(rounded[: entry.shape[0]], reader, TN)
        read_dot = mm(rounded, jnp.concatenate([reader_dot, reader], 0), TN)
        for h in range(width // HEAD_DIM):
            rows = slice(h * HEAD_DIM, (h + 1) * HEAD_DIM)
            e = table[CUM_EXP + h : CUM_EXP + h + 1, lanes]
            d = table[CUM_DOT + h : CUM_DOT + h + 1, lanes]
            inner[rows, lanes] = (within[rows, lanes] + e * read[rows]).astype(BF16)
            inner_dot[rows, lanes] = (
                within_dot[rows, lanes] + e * (read_dot[rows] + d * read[rows])
            ).astype(BF16)
        if b == 0:
            retain, slope = vec[0:1, :], vec[1:2, :]
            entry_dot = retain * (entry_dot + slope * entry) + s0_dot[...]
            entry = retain * entry + s0[...]


def total_body(*refs):
    out = refs[-1]
    summed = refs[0][...].astype(F32)
    for ref in refs[1:-1]:
        summed = summed + ref[...].astype(F32)
    out[...] = summed.astype(BF16)


def on_device(
    tokens,
    tangent_tokens,
    log_decay,
    tangent_decay,
    w_inner,
    w_bmat,
    w_cmat,
    conv_inner,
    conv_bc,
    skip_gain,
    w_out,
):
    length, piece = tokens.shape
    model, width = w_inner.shape
    state_len = w_bmat.shape[1]
    channels = width + 2 * state_len
    heads = width // HEAD_DIM
    n_ctx, n_head = lax.axis_size("ctx"), lax.axis_size("head")
    chips = n_head // 2
    margin = conv_inner.shape[0] - 1
    shape = jax.ShapeDtypeStruct
    place = lax.axis_index("head")

    def along(values, distance):
        route = [
            (2 * i + j, 2 * ((i + distance) % chips) + j) for i in range(chips) for j in range(2)
        ]
        return lax.ppermute(values, "head", route)

    def swap(values):
        return lax.ppermute(values, "head", [(i, i ^ 1) for i in range(n_head)])

    def exchange(values):
        blocks = values.reshape(n_ctx, values.shape[0] // n_ctx, values.shape[1])
        return lax.all_to_all(blocks, "ctx", 0, 0).reshape(values.shape)

    first, second = tokens.T, tangent_tokens.T
    first_up, first_down = along(first, 1), along(first, -1)

    second_down = along(second, -1)
    pad = ((0, 16 - heads), (0, 0))
    dec = jnp.concatenate([jnp.pad(log_decay.T, pad), jnp.pad(tangent_decay.T, pad)], 0)
    table, columns, vec, tail = call(
        decay_body,
        [shape((80, length), F32), shape((length, 32), F32)]
        + [shape((8, width), F32), shape((8, 128), F32)],
        count=1,
        work=(10**8, 10**6),
    )(dec)
    first_up, table = lax.optimization_barrier((first_up, table))
    first_far = along(first_up, 1)
    later, first_far = lax.optimization_barrier((second, first_far))
    second_up = along(later, 1)
    second_far = along(second_down, -1)
    firsts = [first, first_up, first_down, first_far]
    firsts = firsts + [swap(v) for v in firsts]
    here = place[None]
    taps = jnp.concatenate([conv_inner, conv_bc], 1)

    full = [pltpu.VMEM((model, length), BF16), pltpu.VMEM((model, channels), BF16)]
    full += [pltpu.VMEM((length, channels), F32)]
    work = (2 * channels * model * length, 12 * MIB)
    tokens_by = shape((length, channels), BF16)
    (projected,) = call(
        primal_body,
        [tokens_by],
        [*full, pltpu.SemaphoreType.DMA((14,))],
        held=tuple(range(1, 12)),
        loose=tuple(range(2, 9)),
        count=12,
        smem=(0,),
        work=work,
        limit=BIG,
    )(here, *firsts, w_inner, w_bmat, w_cmat)
    second_up, second_far, projected = lax.optimization_barrier(
        (second_up, second_far, projected)
    )
    seconds = [second, second_up, second_down, second_far]
    seconds = seconds + [swap(second), swap(second_up), swap(second_down), swap(second_far)]
    projected_dot, edge = call(
        tangent_body,
        [tokens_by, shape((16, channels), BF16)],
        [*full, pltpu.VMEM((16, channels), BF16), pltpu.SemaphoreType.DMA((15,))],
        near=(12,),
        held=tuple(range(1, 13)),
        loose=tuple(range(2, 9)),
        count=13,
        smem=(0,),
        work=work,
        limit=BIG,
    )(here, *seconds, w_inner, w_bmat, w_cmat, projected)
    before = lax.ppermute(edge, "ctx", [(i, i + 1) for i in range(n_ctx - 1)])
    mix = shape((channels, SPAN), BF16)
    state = shape((state_len, width), F32)

    def block(b, out, *more):
        args = (projected, projected_dot, taps, table, vec, tail, *more)
        return call(
            functools.partial(block_body, b),
            [mix, mix, state, state, *out],
            [pltpu.VMEM((SPAN + 8, channels), F32)] * 2
            + [pltpu.VMEM((SPAN, channels), F32)]
            + [pltpu.VMEM((SPAN, channels), BF16)] * 2
            + [pltpu.VMEM((width, 2 * SPAN), BF16)],
            near=tuple(range(9)),
            pinned=(0, 1, 2, 3, 4) if out else (0, 1),
            count=len(args),
            work=(10**9, 8 * MIB),
            limit=20,
        )(*args)

    mixed1, mixed1_dot, state1, state1_dot = block(1, [])
    mixed0, mixed0_dot, state0, state0_dot, message = block(
        0, [shape((2 * state_len, width + 128), BF16)], before, state1, state1_dot
    )

    arrived = exchange(message)
    gains = jnp.pad(skip_gain[None], ((0, 0), (0, 16 - heads)))
    wide = shape((width, length), F32)
    within, within_dot = call(
        within_body,
        [wide, wide],
        [pltpu.VMEM((SPAN, SPAN), F32)] * 2,
        pinned=True,
        count=7,
        work=(5 * 10**9, 8 * MIB),
        limit=BIG,
    )(mixed0, mixed1, mixed0_dot, mixed1_dot, table, columns, gains)
    half = (lax.axis_index("ctx") % 2).astype(jnp.int32)[None]
    line = pltpu.VMEM((n_ctx, width // 2), F32)
    (leaving,) = call(
        scan_body,
        [shape((2 * state_len, width), BF16)],
        [pltpu.VMEM((2 * state_len, width), F32), line, line],
        near=(1,),
        count=2,
        smem=(0,),
        work=(10**8, MIB),
    )(half, arrived)
    entry = exchange(leaving)

    side = shape((model // 2, width), BF16)
    keep, send = call(
        arrange_body, [side, side], near=(1,), count=2, smem=(0,), work=(10**6, 6 * MIB)
    )(here, w_out.T)
    received = swap(send)
    values = shape((width, length), BF16)
    reader = pltpu.VMEM((state_len, length), BF16)
    inner, inner_dot = call(
        read_body,
        [values, values],
        [reader, reader, pltpu.SemaphoreType.DMA((4,))],
        near=(0,),
        held=(1, 2, 3, 4),
        count=11,
        work=(10**9, 6 * MIB),
        limit=BIG,
    )(
        entry, mixed0, mixed1, mixed0_dot, mixed1_dot, within, within_dot, table, vec, state0,
        state0_dot,
    )
    term = shape((piece, length), BF16)
    work = (2 * chips * piece * width * length, 4 * MIB)
    begin = call(
        own_body, [shape((chips * piece, length), F32)], near=(0, 1), count=2, work=work
    )
    product = call(product_body, [term] * chips, near=(0, 1, 2), count=3, work=work)

    def total(*terms):
        count = len(terms)
        body = call(total_body, [term], near=range(count), count=count, work=(10**6, 2 * MIB))
        return body(*terms)[0]

    def finish(begun, other, way):
        terms = product(begun, received, other)
        far = along(terms[2], way)
        near, back = (terms[1], terms[3]) if way == 1 else (terms[3], terms[1])
        back = along(back, -way)
        near = along(total(near, far), way)
        return total(terms[0], near, back).T

    other, other_dot = swap(inner), swap(inner_dot)
    begun, begun_dot = begin(keep, inner)[0], begin(keep, inner_dot)[0]
    return finish(begun, other, 1), finish(begun_dot, other_dot, -1)


def solution(mesh):
    in_specs = (
        P("ctx", "head"),
        P("ctx", "head"),
        P("ctx", "head"),
        P("ctx", "head"),
        P(None, "head"),
        P(),
        P(),
        P(None, "head"),
        P(),
        P("head"),
        P("head", None),
    )
    out_specs = (P("ctx", "head"), P("ctx", "head"))
    return jax.shard_map(
        on_device, mesh=mesh, in_specs=in_specs, out_specs=out_specs, check_vma=False
    )
```

```python
import functools

import jax
import jax.numpy as jnp
from jax import lax
from jax.experimental import pallas as pl
from jax.experimental.pallas import tpu as pltpu
from jax.sharding import PartitionSpec as P

HEAD_DIM = 64
SPAN = 256
MIB = 1 << 20
BIG = 24
CHIPS = 4
AROUND = (0, CHIPS - 1, 1, 2)
BF16 = jnp.bfloat16
F32 = jnp.float32
HIGHEST = lax.Precision.HIGHEST

NN = (((1,), (0,)), ((), ()))
NT = (((1,), (1,)), ((), ()))
TN = (((0,), (0,)), ((), ()))


def mm(a, b, dims=NN, precision=None):
    return lax.dot_general(a, b, dims, precision=precision, preferred_element_type=F32)


def call(body, out, scratch=(), smem=(), near=(), held=(), loose=(), pinned=(), count=0, work=(0, 0), limit=16):
    outs = list(out)
    n_out, n_scratch = len(outs), len(scratch)
    far = [i for i in range(count) if i not in smem and i not in held and i not in near]
    far_out = list(range(n_out)) if pinned is True else list(pinned)

    def kernel(*refs):
        ins, res = list(refs[:count]), list(refs[count : count + n_out])
        rest = refs[count + n_out :]
        own, rest = list(rest[:n_scratch]), list(rest[n_scratch:])
        copies, late = [], []
        for k, i in enumerate(far):
            copies.append(pltpu.make_async_copy(ins[i], rest[k], rest[-1].at[k]))
            ins[i] = rest[k]
        for k, i in enumerate(far_out, len(far)):
            late.append(pltpu.make_async_copy(rest[k], res[i], rest[-1].at[k]))
            res[i] = rest[k]
        for copy in copies:
            copy.start()
        if held:
            body(copies, *ins, *res, *own)
        else:
            for copy in copies:
                copy.wait()
            body(*ins, *res, *own)
        for copy in late:
            copy.start()
        for copy in late:
            copy.wait()

    def space(i):
        if i in smem:
            return pltpu.SMEM
        return pltpu.VMEM if i in near else pl.ANY if i in loose else pltpu.HBM

    def run(*args):
        assert len(args) == count
        buffers = [pltpu.VMEM(args[i].shape, args[i].dtype) for i in far]
        args = [
            pltpu.with_memory_space_constraint(v, pltpu.HBM) if space(i) is pltpu.HBM else v
            for i, v in enumerate(args)
        ]
        buffers += [pltpu.VMEM(outs[i].shape, outs[i].dtype) for i in far_out]
        if buffers:
            buffers.append(pltpu.SemaphoreType.DMA((len(buffers),)))
        return pl.pallas_call(
            kernel,
            out_shape=[
                pltpu.HBM(v.shape, v.dtype) if i in far_out else v for i, v in enumerate(outs)
            ],
            in_specs=[pl.BlockSpec(memory_space=space(i)) for i in range(count)],
            out_specs=[
                pl.BlockSpec(memory_space=pltpu.HBM if i in far_out else pltpu.VMEM)
                for i in range(n_out)
            ],
            scratch_shapes=list(scratch) + buffers,
            cost_estimate=pl.CostEstimate(
                flops=work[0], bytes_accessed=work[1], transcendentals=0
            ),
            compiler_params=pltpu.CompilerParams(vmem_limit_bytes=limit * MIB),
        )(*args)

    return run


def spread(rows, width):
    head = lax.broadcasted_iota(jnp.int32, (rows, width), 0)
    lane = lax.broadcasted_iota(jnp.int32, (rows, width), 1)
    return jnp.where(lane // HEAD_DIM == head, 1.0, 0.0).astype(F32)


CUM, CUM_DOT, REM, REM_DOT, CUM_EXP = 0, 16, 32, 48, 64


def decay_body(dec, table, columns, vec, tail):
    s = lax.broadcasted_iota(jnp.int32, (SPAN, SPAN), 0)
    t = lax.broadcasted_iota(jnp.int32, (SPAN, SPAN), 1)
    upper = jnp.where(s <= t, 1.0, 0.0).astype(F32)
    lower = jnp.where(t <= s, 1.0, 0.0).astype(F32)
    ends = []
    for b in range(dec.shape[1] // SPAN):
        lanes = slice(b * SPAN, (b + 1) * SPAN)
        both = dec[:, lanes]
        c = mm(both, upper, NN, HIGHEST)
        c_t = mm(lower, both, NT, HIGHEST)
        p, d = c[:16], c[16:]
        table[CUM : CUM + 16, lanes] = p
        table[CUM_DOT : CUM_DOT + 16, lanes] = d
        table[CUM_EXP : CUM_EXP + 16, lanes] = jnp.exp(p)
        r = jnp.exp(p[:, SPAN - 1 :] - p)
        table[REM : REM + 16, lanes] = r
        table[REM_DOT : REM_DOT + 16, lanes] = r * (d[:, SPAN - 1 :] - d)
        columns[lanes, :] = c_t
        ends.append(c_t[SPAN - 1 :, :])
    rows = jnp.concatenate(
        [ends[0][:, :16], ends[0][:, 16:], ends[1][:, :16], ends[1][:, 16:]]
        + [jnp.zeros((4, 16), F32)],
        0,
    )
    wide = mm(rows, spread(16, vec.shape[1]), NN, HIGHEST)
    row = lax.broadcasted_iota(jnp.int32, wide.shape, 0)
    vec[...] = jnp.where((row == 0) | (row == 2), jnp.exp(wide), wide)
    rest = ends[0] + ends[1]
    tail[...] = jnp.zeros(tail.shape, F32)
    for i in range(3):
        term = rest.astype(BF16).astype(F32)
        tail[i : i + 1, 0:32] = term
        rest = rest - term


def group(place, distance, other):
    chip, core = place[0] // 2, place[0] % 2
    return (chip + distance) % CHIPS * 2 + (1 - core if other else core)


def gather(place, pieces, full, sems):
    rows = pieces[0].shape[0]
    arriving = []
    for i, piece in enumerate(pieces):
        at = group(place, AROUND[i % 4], i >= 4) * rows
        here = full.at[pl.ds(pl.multiple_of(at, rows), rows), :]
        arriving.append(pltpu.make_async_copy(piece, here, sems.at[i]))
    for copy in arriving:
        copy.start()
    return arriving


CHUNK = 64


def convolve(ext, taps, store):
    count = taps.shape[0]
    for c in range(taps.shape[1] // 128):
        lanes = slice(c * 128, (c + 1) * 128)
        kernel = [jnp.broadcast_to(taps[k : k + 1, lanes], (CHUNK, 128)) for k in range(count)]
        for r in range(0, SPAN, CHUNK):
            summed = None
            for k in range(count):
                at = r + 9 - count + k
                term = kernel[k] * ext[at : at + CHUNK, lanes]
                summed = term if summed is None else summed + term
            store(slice(r, r + CHUNK), lanes, summed)


def turn(rows):
    s = lax.broadcasted_iota(jnp.int32, (SPAN, SPAN), 0)
    t = lax.broadcasted_iota(jnp.int32, (SPAN, SPAN), 1)
    return mm(rows, jnp.where(s == t, 1.0, 0.0).astype(BF16), TN).astype(BF16)


def to_owners(values):
    n, width = values.shape
    halves = [values[:, : width // 2], values[:, width // 2 :]]
    stacked = jnp.stack([v.reshape(n // 8, 8, width // 2) for v in halves], 1)
    return stacked.reshape(2 * n, width // 2)


def from_owners(values):
    n, width = values.shape
    split = values.reshape(n // 16, 2, 8, width)
    return jnp.concatenate([split[:, i].reshape(n // 2, width) for i in range(2)], 1)


def project(place, pieces, weights, out, full, w_all, total, sems):
    arriving = gather(place, pieces, full, sems)
    half = w_all.shape[0] // 2
    coming = []
    for part in range(2):
        rows = slice(part * half, (part + 1) * half)
        at = 0
        for i, weight in enumerate(weights):
            columns = slice(at, at + weight.shape[1])
            at = columns.stop
            copy = pltpu.make_async_copy(
                weight.at[rows, :], w_all.at[rows, columns], sems.at[8 + 3 * part + i]
            )
            copy.start()
            coming.append(copy)
    for copy in [*arriving, *coming[:3]]:
        copy.wait()
    total[...] = mm(full[:half, :], w_all[:half, :], TN)
    for copy in coming[3:]:
        copy.wait()
    out[...] = (total[...] + mm(full[half:, :], w_all[half:, :], TN)).astype(BF16)


def primal_body(copies, place, *refs):
    project(place, refs[:8], refs[8:11], *refs[11:])


def tangent_body(copies, place, *refs):
    first, projected, edge, full, w_all, total, last, sems = refs[11:]
    length = full.shape[1]
    ending = pltpu.make_async_copy(first.at[length - 16 :, :], last, sems.at[14])
    ending.start()
    project(place, refs[:8], refs[8:11], projected, full, w_all, total, sems)
    ending.wait()
    ends = [last[...].astype(F32)[8:], projected[length - 16 :, :].astype(F32)[8:]]
    edge[...] = jnp.concatenate(ends, 0).astype(BF16)


def block_body(b, projected, projected_dot, taps, table, vec, tail, *refs):
    if b == 0:
        before, state1, state1_dot, mixed, mixed_dot, state, state_dot, message = refs[:8]
        refs = refs[8:]
    else:
        mixed, mixed_dot, state, state_dot = refs[:4]
        refs = refs[4:]
    ext, ext_dot, gate, rows, rows_dot, scaled = refs
    at = slice(b * SPAN, (b + 1) * SPAN)
    for i, (source, out) in enumerate(((projected, ext), (projected_dot, ext_dot))):
        if b > 0:
            ahead = source[b * SPAN - 16 : b * SPAN, :].astype(F32)[8:]
        else:
            ahead = before[...].astype(F32)[8 * i : 8 * i + 8]
        out[0:8, :] = ahead
        out[8:, :] = source[at, :].astype(F32)

    def store(where, lanes, v):
        sig = 0.5 + 0.5 * jnp.tanh(0.5 * v)
        rows[where, lanes] = (v * sig).astype(BF16)
        gate[where, lanes] = sig * (1.0 + v * (1.0 - sig))

    def store_dot(where, lanes, v):
        rows_dot[where, lanes] = (gate[where, lanes] * v).astype(BF16)

    convolve(ext, taps, store)
    mixed[...] = turn(rows[...])
    convolve(ext_dot, taps, store_dot)
    mixed_dot[...] = turn(rows_dot[...])
    width = vec.shape[1]
    for h in range(width // HEAD_DIM):
        here = slice(h * HEAD_DIM, (h + 1) * HEAD_DIM)
        value = mixed[here, :].astype(F32)
        r = table[REM + h : REM + h + 1, at]
        scaled[here, SPAN:] = (value * r).astype(BF16)
        scaled[here, :SPAN] = (
            mixed_dot[here, :].astype(F32) * r + value * table[REM_DOT + h : REM_DOT + h + 1, at]
        ).astype(BF16)
    writer = mixed[width : width + 128, :]
    writer_dot = mixed_dot[width : width + 128, :]
    own = mm(writer, scaled[:, SPAN:], NT)
    own_dot = mm(jnp.concatenate([writer, writer_dot], 1), scaled[...], NT)
    state[...] = own
    state_dot[...] = own_dot
    if b == 0:
        own_dot = vec[2:3, :] * (own_dot + vec[3:4, :] * own) + state1_dot[...]
        own = vec[2:3, :] * own + state1[...]
        message[:, : width // 2] = to_owners(own).astype(BF16)
        message[:, width // 2 : width] = to_owners(own_dot).astype(BF16)
        both = jnp.concatenate([tail[...], tail[...]], 0).astype(BF16)
        for j in range(message.shape[0] // 16):
            message[16 * j : 16 * j + 16, width:] = both


def within_body(first, second, first_dot, second_dot, table, columns, gain, within, within_dot, sc, scd):
    width = within.shape[0]
    state = (first.shape[0] - width) // 2
    s = lax.broadcasted_iota(jnp.int32, (SPAN, SPAN), 0)
    t = lax.broadcasted_iota(jnp.int32, (SPAN, SPAN), 1)
    causal = s <= t
    for b in range(2):
        lanes = slice(b * SPAN, (b + 1) * SPAN)
        mixed, mixed_dot = ((first, first_dot), (second, second_dot))[b]
        writer, reader = mixed[width : width + state, :], mixed[width + state :, :]
        writer_dot, reader_dot = mixed_dot[width : width + state, :], mixed_dot[width + state :, :]
        sc[...] = mm(writer, reader, TN)
        scd[...] = mm(jnp.concatenate([writer_dot, writer], 0), jnp.concatenate([reader, reader_dot], 0), TN)
        for h in range(width // HEAD_DIM):
            rows = slice(h * HEAD_DIM, (h + 1) * HEAD_DIM)
            diff = table[CUM + h : CUM + h + 1, lanes] - columns[lanes, h : h + 1]
            diff_dot = (
                table[CUM_DOT + h : CUM_DOT + h + 1, lanes] - columns[lanes, 16 + h : 17 + h]
            )
            weight = jnp.exp(jnp.where(causal, diff, -jnp.inf))
            mix = (weight * sc[...]).astype(BF16)
            mix_dot = (weight * (scd[...] + diff_dot * sc[...])).astype(BF16)
            value, value_dot = mixed[rows, :], mixed_dot[rows, :]
            both = mm(jnp.concatenate([value, value_dot], 0), mix)
            other = mm(value, mix_dot)
            skip = gain[0:1, h : h + 1]
            within[rows, lanes] = both[:HEAD_DIM] + skip * value.astype(F32)
            within_dot[rows, lanes] = (both[HEAD_DIM:] + other) + skip * value_dot.astype(F32)


def unpack(half, width, which):
    lane = lax.broadcasted_iota(jnp.int32, (128, width), 0)
    head = lax.broadcasted_iota(jnp.int32, (128, width), 1) // HEAD_DIM + half * (width // HEAD_DIM)
    return jnp.where(lane == head + 16 * which, 1.0, 0.0).astype(BF16)


def scan_body(half, arrived, leaving, states, retain, slope):
    rows, whole = 8, leaving.shape[1]
    width = whole // 2
    steps = arrived.shape[0] // rows
    tails = arrived[:, whole:]
    for which, out in ((0, retain), (1, slope)):
        terms = mm(tails, unpack(half[0], width, which)).reshape(steps, rows, width)
        out[...] = (terms[:, 0] + terms[:, 1]) + terms[:, 2]
    retain[...] = jnp.exp(retain[...])
    states[...] = arrived[:, :whole].astype(F32)
    state = jnp.zeros((rows, width), F32)
    state_dot = jnp.zeros((rows, width), F32)
    for j in range(steps):
        own = slice(j * rows, (j + 1) * rows)
        arriving, arriving_dot = states[own, :width], states[own, width:]
        states[own, :width] = state
        states[own, width:] = state_dot
        r = retain[j : j + 1, :]
        state_dot = r * (state_dot + slope[j : j + 1, :] * state) + arriving_dot
        state = r * state + arriving
    leaving[...] = states[...].astype(BF16)


def arrange_body(place, w_t, keep, send):
    rows = w_t.shape[0] // (2 * CHIPS)
    for d in range(CHIPS):
        own = slice(d * rows, (d + 1) * rows)
        for other, out in ((False, keep), (True, send)):
            at = pl.multiple_of(group(place, d, other) * rows, rows)
            out[own, :] = w_t[pl.ds(at, rows), :]


def own_body(keep, own, out):
    for b in range(own.shape[1] // SPAN):
        lanes = slice(b * SPAN, (b + 1) * SPAN)
        out[:, lanes] = mm(keep[...], own[:, lanes])


def product_body(begun, received, other, *outs):
    rows = outs[0].shape[0]
    for b in range(other.shape[1] // SPAN):
        lanes = slice(b * SPAN, (b + 1) * SPAN)
        result = begun[:, lanes] + mm(received[...], other[:, lanes])
        for d, out in enumerate(outs):
            out[:, lanes] = result[d * rows : (d + 1) * rows].astype(BF16)


def read_body(
    copies, arrived, first, second, first_dot, second_dot, within, within_dot, table, vec, s0, s0_dot,
    inner, inner_dot, readers, readers_dot, sems,
):
    n = readers.shape[0]
    reading = []
    for i, (source, out) in enumerate(
        ((first, readers), (second, readers), (first_dot, readers_dot), (second_dot, readers_dot))
    ):
        lanes = slice((i % 2) * SPAN, (i % 2 + 1) * SPAN)
        reading.append(
            pltpu.make_async_copy(
                source.at[source.shape[0] - n :, :], out.at[:, lanes], sems.at[i]
            )
        )
    for copy in reading:
        copy.start()
    for copy in [*copies, *reading]:
        copy.wait()
    width = within.shape[0]
    entry = from_owners(arrived[:, : width // 2].astype(F32))
    entry_dot = from_owners(arrived[:, width // 2 :].astype(F32))
    for b in range(2):
        lanes = slice(b * SPAN, (b + 1) * SPAN)
        reader, reader_dot = readers[:, lanes], readers_dot[:, lanes]
        rounded = jnp.concatenate([entry.astype(BF16), entry_dot.astype(BF16)], 0)
        read = mm(rounded[: entry.shape[0]], reader, TN)
        read_dot = mm(rounded, jnp.concatenate([reader_dot, reader], 0), TN)
        for h in range(width // HEAD_DIM):
            rows = slice(h * HEAD_DIM, (h + 1) * HEAD_DIM)
            e = table[CUM_EXP + h : CUM_EXP + h + 1, lanes]
            d = table[CUM_DOT + h : CUM_DOT + h + 1, lanes]
            inner[rows, lanes] = (within[rows, lanes] + e * read[rows]).astype(BF16)
            inner_dot[rows, lanes] = (
                within_dot[rows, lanes] + e * (read_dot[rows] + d * read[rows])
            ).astype(BF16)
        if b == 0:
            retain, slope = vec[0:1, :], vec[1:2, :]
            entry_dot = retain * (entry_dot + slope * entry) + s0_dot[...]
            entry = retain * entry + s0[...]


def total_body(*refs):
    out = refs[-1]
    summed = refs[0][...].astype(F32)
    for ref in refs[1:-1]:
        summed = summed + ref[...].astype(F32)
    out[...] = summed.astype(BF16)


def on_device(
    tokens,
    tangent_tokens,
    log_decay,
    tangent_decay,
    w_inner,
    w_bmat,
    w_cmat,
    conv_inner,
    conv_bc,
    skip_gain,
    w_out,
):
    length, piece = tokens.shape
    model, width = w_inner.shape
    state_len = w_bmat.shape[1]
    channels = width + 2 * state_len
    heads = width // HEAD_DIM
    n_ctx, n_head = lax.axis_size("ctx"), lax.axis_size("head")
    chips = n_head // 2
    margin = conv_inner.shape[0] - 1
    shape = jax.ShapeDtypeStruct
    place = lax.axis_index("head")

    def along(values, distance):
        route = [
            (2 * i + j, 2 * ((i + distance) % chips) + j) for i in range(chips) for j in range(2)
        ]
        return lax.ppermute(values, "head", route)

    def swap(values):
        return lax.ppermute(values, "head", [(i, i ^ 1) for i in range(n_head)])

    def exchange(values):
        blocks = values.reshape(n_ctx, values.shape[0] // n_ctx, values.shape[1])
        return lax.all_to_all(blocks, "ctx", 0, 0).reshape(values.shape)

    first, second = tokens.T, tangent_tokens.T
    first_up, first_down = along(first, 1), along(first, -1)

    second_down = along(second, -1)
    pad = ((0, 16 - heads), (0, 0))
    dec = jnp.concatenate([jnp.pad(log_decay.T, pad), jnp.pad(tangent_decay.T, pad)], 0)
    table, columns, vec, tail = call(
        decay_body,
        [shape((80, length), F32), shape((length, 32), F32)]
        + [shape((8, width), F32), shape((8, 128), F32)],
        count=1,
        work=(10**8, 10**6),
    )(dec)
    first_up, table = lax.optimization_barrier((first_up, table))
    first_far = along(first_up, 1)
    later, first_far = lax.optimization_barrier((second, first_far))
    second_up = along(later, 1)
    firsts = [first, first_up, first_down, first_far]
    firsts = firsts + [swap(v) for v in firsts]
    second_down, firsts[-1] = lax.optimization_barrier((second_down, firsts[-1]))
    second_far = along(second_down, -1)
    here = place[None]
    taps = jnp.concatenate([conv_inner, conv_bc], 1)

    full = [pltpu.VMEM((model, length), BF16), pltpu.VMEM((model, channels), BF16)]
    full += [pltpu.VMEM((length, channels), F32)]
    work = (2 * channels * model * length, 12 * MIB)
    tokens_by = shape((length, channels), BF16)
    (projected,) = call(
        primal_body,
        [tokens_by],
        [*full, pltpu.SemaphoreType.DMA((14,))],
        held=tuple(range(1, 12)),
        loose=tuple(range(2, 9)),
        count=12,
        smem=(0,),
        work=work,
        limit=BIG,
    )(here, *firsts, w_inner, w_bmat, w_cmat)
    second_up, second_far, projected = lax.optimization_barrier(
        (second_up, second_far, projected)
    )
    seconds = [second, second_up, second_down, second_far]
    seconds = seconds + [swap(second), swap(second_up), swap(second_down), swap(second_far)]
    projected_dot, edge = call(
        tangent_body,
        [tokens_by, shape((16, channels), BF16)],
        [*full, pltpu.VMEM((16, channels), BF16), pltpu.SemaphoreType.DMA((15,))],
        near=(12,),
        held=tuple(range(1, 13)),
        loose=tuple(range(2, 9)),
        count=13,
        smem=(0,),
        work=work,
        limit=BIG,
    )(here, *seconds, w_inner, w_bmat, w_cmat, projected)
    before = lax.ppermute(edge, "ctx", [(i, i + 1) for i in range(n_ctx - 1)])
    mix = shape((channels, SPAN), BF16)
    state = shape((state_len, width), F32)

    def block(b, out, *more):
        args = (projected, projected_dot, taps, table, vec, tail, *more)
        return call(
            functools.partial(block_body, b),
            [mix, mix, state, state, *out],
            [pltpu.VMEM((SPAN + 8, channels), F32)] * 2
            + [pltpu.VMEM((SPAN, channels), F32)]
            + [pltpu.VMEM((SPAN, channels), BF16)] * 2
            + [pltpu.VMEM((width, 2 * SPAN), BF16)],
            near=tuple(range(9)),
            pinned=(0, 1, 2, 3, 4) if out else (0, 1),
            count=len(args),
            work=(10**9, 8 * MIB),
            limit=20,
        )(*args)

    mixed1, mixed1_dot, state1, state1_dot = block(1, [])
    mixed0, mixed0_dot, state0, state0_dot, message = block(
        0, [shape((2 * state_len, width + 128), BF16)], before, state1, state1_dot
    )

    arrived = exchange(message)
    gains = jnp.pad(skip_gain[None], ((0, 0), (0, 16 - heads)))
    wide = shape((width, length), F32)
    within, within_dot = call(
        within_body,
        [wide, wide],
        [pltpu.VMEM((SPAN, SPAN), F32)] * 2,
        pinned=True,
        count=7,
        work=(5 * 10**9, 8 * MIB),
        limit=BIG,
    )(mixed0, mixed1, mixed0_dot, mixed1_dot, table, columns, gains)
    half = (lax.axis_index("ctx") % 2).astype(jnp.int32)[None]
    line = pltpu.VMEM((n_ctx, width // 2), F32)
    (leaving,) = call(
        scan_body,
        [shape((2 * state_len, width), BF16)],
        [pltpu.VMEM((2 * state_len, width), F32), line, line],
        near=(1,),
        count=2,
        smem=(0,),
        work=(10**8, MIB),
    )(half, arrived)
    entry = exchange(leaving)

    side = shape((model // 2, width), BF16)
    keep, send = call(
        arrange_body, [side, side], near=(1,), count=2, smem=(0,), work=(10**6, 6 * MIB)
    )(here, w_out.T)
    received = swap(send)
    values = shape((width, length), BF16)
    reader = pltpu.VMEM((state_len, length), BF16)
    inner, inner_dot = call(
        read_body,
        [values, values],
        [reader, reader, pltpu.SemaphoreType.DMA((4,))],
        near=(0,),
        held=(1, 2, 3, 4),
        count=11,
        work=(10**9, 6 * MIB),
        limit=BIG,
    )(
        entry, mixed0, mixed1, mixed0_dot, mixed1_dot, within, within_dot, table, vec, state0,
        state0_dot,
    )
    term = shape((piece, length), BF16)
    work = (2 * chips * piece * width * length, 4 * MIB)
    begin = call(
        own_body, [shape((chips * piece, length), F32)], near=(0, 1), count=2, work=work
    )
    product = call(product_body, [term] * chips, near=(0, 1, 2), count=3, work=work)

    def total(*terms):
        count = len(terms)
        body = call(total_body, [term], near=range(count), count=count, work=(10**6, 2 * MIB))
        return body(*terms)[0]

    def finish(begun, other, way):
        terms = product(begun, received, other)
        far = along(terms[2], way)
        near, back = (terms[1], terms[3]) if way == 1 else (terms[3], terms[1])
        back = along(back, -way)
        near = along(total(near, far), way)
        return total(terms[0], near, back).T

    other, other_dot = swap(inner), swap(inner_dot)
    begun, begun_dot = begin(keep, inner)[0], begin(keep, inner_dot)[0]
    return finish(begun, other, 1), finish(begun_dot, other_dot, -1)


def solution(mesh):
    in_specs = (
        P("ctx", "head"),
        P("ctx", "head"),
        P("ctx", "head"),
        P("ctx", "head"),
        P(None, "head"),
        P(),
        P(),
        P(None, "head"),
        P(),
        P("head"),
        P("head", None),
    )
    out_specs = (P("ctx", "head"), P("ctx", "head"))
    return jax.shard_map(
        on_device, mesh=mesh, in_specs=in_specs, out_specs=out_specs, check_vma=False
    )
```
